32 devices in a mesh: pp: 4 (over y, core), ep: 8 (over z, x).
Axes of the slice: x: 2, y: 2, z: 4, core: 2. Of those that a mesh axis runs over, the one named last changes fastest.
Arguments:
- fwd_in: bfloat16 [4, 1024, 3584], P('pp', 'ep'), may hold values from -6 to 6
- fwd_ids: int32 [4, 1024, 1], P('pp', 'ep'), may hold values from 0 to 7; in each aligned block of 128 rows (0 to 127, 128 to 255, ..., all dimensions but the last counted through in order) at most 20 rows name the same one
- saved_in: bfloat16 [4, 1024, 3584], P('pp', 'ep'), may hold values from -6 to 6
- bwd_ids: int32 [4, 1024, 1], P('pp', 'ep'), may hold values from 0 to 7; in each aligned block of 128 rows (0 to 127, 128 to 255, ..., all dimensions but the last counted through in order) at most 20 rows name the same one
- grad_in: bfloat16 [4, 1024, 3584], P('pp', 'ep'), may hold values from -6 to 6
- router: float32 [4, 3584, 8], P('pp'), may hold values from -0.09375 to 0.09375
- w_gate: bfloat16 [4, 3584, 8192], P('pp', None, 'ep'), may hold values from -0.09375 to 0.09375
- w_up: bfloat16 [4, 3584, 8192], P('pp', None, 'ep'), may hold values from -0.09375 to 0.09375
- w_down: bfloat16 [4, 8192, 3584], P('pp', 'ep'), may hold values from -0.1875 to 0.1875
Outputs:
- fwd_next: bfloat16 [4, 1024, 3584], P('pp', 'ep')
- grad_next: bfloat16 [4, 1024, 3584], P('pp', 'ep')
The draws below stay inside these ranges and needn't reach their ends.
Inputs may be any that keep to these rules, and one draw needn't show every extreme that they name: `fwd_ids`: within the 128 tokens of one device's aligned block, no expert is chosen more than 20 times; some block chooses some expert exactly 20 times. `bwd_ids`: as for fwd_ids.
All inputs are finite; a program needn't handle non-finite values.
Results may differ from the reference program's by a relative error of at most 0.011.
Values may be sent and summed in bfloat16 or wider, within the bound.
No kernel may reach another device: no remote copies, remote signals or barrier semaphores. Data moves between devices by JAX's collectives and lax.ppermute only.
A program may use at most 128 MiB of HBM per device.

```python
import math
import jax
import jax.numpy as jnp
import numpy as np
from jax import lax

D = 3584
FF = 1024
EXPERTS = 8
TOPK = 1
TOK_DEV = 128
SPAN = 1
FF_DEV = 1024
CAP = 20
TOKENS = 1024
N_PP = 4
N_EP = 8


def block_scale(stream_key, dims, shards, least, largest):
    def one(axis_at, blocks):
        steps = jax.random.uniform(jax.random.fold_in(jax.random.fold_in(stream_key, 6), axis_at), (blocks,), jnp.float32, least / len(shards), largest / len(shards))
        return jnp.repeat(jnp.exp(steps), dims[axis_at] // blocks).reshape((-1,) + (1,) * (len(dims) - axis_at - 1))

    loudness = one(*shards[0])
    for cut in shards[1:]:
        loudness = loudness * one(*cut)
    return loudness


def routed_block(own_key, own, number, rows, count, top, bound, lean):
    order = jax.random.permutation(own_key, count)
    crowded, ordinary = shares(count, rows * top, bound, lean, True), shares(count, rows * top, bound, lean, False)
    places = jnp.arange(count)

    def named(lengths, offset_by):
        used = int((lengths > 0).sum())
        fixed = max(1, used // 4)
        passed = fixed + (places - fixed + offset_by * (used - fixed)) % max(1, count - fixed)
        return jnp.zeros((count,), jnp.int32).at[order[jnp.where(places < fixed, places, passed)]].set(jnp.asarray(lengths, jnp.int32))

    lengths = jnp.where(number % 4 == 0, named(crowded, number // 4), named(ordinary, number - number // 4 - 1))
    mixed = jax.random.permutation(jax.random.fold_in(own, 3), count)
    giver, receiver = mixed[0:count // 2 * 2:2], mixed[1:count // 2 * 2:2]
    slack = jnp.minimum(lengths[giver] - 1, bound - lengths[receiver]) // 2
    slack = jnp.where((giver == order[0]) | (receiver == order[0]) | (lengths[receiver] == 0), 0, jnp.maximum(slack, 0))
    passed = jax.random.randint(jax.random.fold_in(own, 4), (count // 2,), 0, 1 << 20) % (slack + 1)
    lengths = lengths.at[giver].add(-passed).at[receiver].add(passed)
    labels = jnp.searchsorted(jnp.cumsum(lengths), jnp.arange(rows * top), side="right").astype(jnp.int32)
    listing = labels.reshape(top, rows).T
    listing = listing[jax.random.permutation(jax.random.fold_in(own, 1), rows)]
    offset_by = jax.random.randint(jax.random.fold_in(own, 2), (rows, 1), 0, top)
    return jnp.take_along_axis(listing, (jnp.arange(top)[None, :] + offset_by) % top, axis=1)


def shares(number_of, total, reach, lean, full):
    portions = [(1 << 20) // math.isqrt(standing ** lean) + 1 for standing in range(1, number_of + 1)]
    largest = reach if full else min(reach, max(-(-total // number_of), total * portions[0] // sum(portions)))
    least = 1 if total - largest >= number_of - 1 else 0
    counts, surplus = [largest] + [least] * (number_of - 1), total - largest - least * (number_of - 1)
    while surplus > 0:
        free = [i for i in range(1, number_of) if counts[i] < largest] or [i for i in range(1, number_of) if counts[i] < reach]
        pool, left = sum([portions[i] for i in free]), surplus
        for i in free:
            more = min(reach - counts[i], max(1, left * portions[i] // pool), surplus)
            counts[i] = counts[i] + more
            surplus = surplus - more
    return np.array(counts)


def scatter_about(stream_key, extent, scale, bound, split=(), kind=jnp.bfloat16):
    loudness = block_scale(stream_key, extent, split, -0.22, 0.18) if split else 1.0
    values = jax.random.normal(stream_key, extent, jnp.float32) * scale * loudness
    return jnp.minimum(jnp.maximum(values, -bound), bound).astype(kind)


def setup_inputs(seed: int = 0) -> dict:
    seeds = jax.random.split(jax.random.key(seed), 10)
    fwd_in = scatter_about(seeds[0], (N_PP, TOKENS, D), 1.0, 6.0, ((0, 4), (1, 8)))
    fwd_ids_keys = jax.random.split(jax.random.fold_in(seeds[1], 1), N_PP * TOKENS // TOK_DEV)
    fwd_ids_turns = jax.random.permutation(jax.random.fold_in(seeds[1], 3), N_PP * TOKENS // TOK_DEV)
    fwd_ids = jax.vmap(lambda own, number: routed_block(jax.random.fold_in(seeds[1], 2), own, number, TOK_DEV, EXPERTS, TOPK, CAP, 2))(fwd_ids_keys, fwd_ids_turns).reshape((N_PP, TOKENS, TOPK))
    saved_in = scatter_about(seeds[2], (N_PP, TOKENS, D), 1.0, 6.0, ((0, 4), (1, 8)))
    bwd_ids_keys = jax.random.split(jax.random.fold_in(seeds[3], 1), N_PP * TOKENS // TOK_DEV)
    bwd_ids_turns = jax.random.permutation(jax.random.fold_in(seeds[3], 3), N_PP * TOKENS // TOK_DEV)
    bwd_ids = jax.vmap(lambda own, number: routed_block(jax.random.fold_in(seeds[3], 2), own, number, TOK_DEV, EXPERTS, TOPK, CAP, 2))(bwd_ids_keys, bwd_ids_turns).reshape((N_PP, TOKENS, TOPK))
    grad_in = scatter_about(seeds[4], (N_PP, TOKENS, D), 1.0, 6.0, ((0, 4), (1, 8)))
    router = scatter_about(seeds[5], (N_PP, D, EXPERTS), D ** -0.5, 0.09375, ((0, 4),), jnp.float32)
    w_gate = scatter_about(seeds[6], (N_PP, D, EXPERTS * FF), D ** -0.5, 0.09375, ((0, 4), (2, 8)))
    w_up = scatter_about(seeds[7], (N_PP, D, EXPERTS * FF), D ** -0.5, 0.09375, ((0, 4), (2, 8)))
    w_down = scatter_about(seeds[8], (N_PP, EXPERTS * FF, D), FF ** -0.5, 0.1875, ((0, 4), (1, 8)))
    return {"fwd_in": fwd_in, "fwd_ids": fwd_ids, "saved_in": saved_in, "bwd_ids": bwd_ids, "grad_in": grad_in, "router": router, "w_gate": w_gate, "w_up": w_up, "w_down": w_down}


route_scale = 2.5
contract = (((1,), (1,)), ((), ()))


def slots_of(chosen):
    blocks = chosen.reshape(N_EP, TOK_DEV)
    onehot = (blocks[:, :, None] == jnp.arange(EXPERTS, dtype=jnp.int32)[None, None, :]).astype(jnp.int32)
    before = jnp.cumsum(onehot, axis=1) - onehot
    ranking = jnp.sum(before * onehot, axis=2)
    slot_index = (jnp.arange(N_EP, dtype=jnp.int32)[:, None] * CAP + ranking).reshape(-1).astype(jnp.int32)
    slot_table = jnp.full((EXPERTS, N_EP * CAP), TOKENS, jnp.int32)
    slot_table = slot_table.at[chosen, slot_index].set(jnp.arange(TOKENS, dtype=jnp.int32))
    return slot_index, slot_table


def routing_weight(tokens, router, chosen):
    logits = jnp.dot(tokens.astype(jnp.float32), router, precision=lax.Precision.HIGHEST)
    picked = jnp.take_along_axis(logits, chosen[:, None], axis=1)[:, 0]
    return route_scale * jax.nn.sigmoid(picked)


def expert_forward(row_block, gate_cols, up_cols, down_rows):
    gate_proj = jnp.dot(row_block, gate_cols, preferred_element_type=jnp.float32)
    up_proj = jnp.dot(row_block, up_cols, preferred_element_type=jnp.float32)
    hidden = (gate_proj * jax.nn.sigmoid(gate_proj) * up_proj).astype(jnp.bfloat16)
    running = jnp.zeros((row_block.shape[0], D), jnp.float32)
    for unit_block in range(SPAN):
        first_unit = unit_block * FF_DEV
        partial_sum = jnp.dot(hidden[:, first_unit:first_unit + FF_DEV], down_rows[first_unit:first_unit + FF_DEV], preferred_element_type=jnp.float32).astype(jnp.bfloat16)
        running = running + partial_sum.astype(jnp.float32)
    return running.astype(jnp.bfloat16)


def expert_backward(row_block, row_grads, gate_cols, up_cols, down_rows):
    gate_proj = jnp.dot(row_block, gate_cols, preferred_element_type=jnp.float32)
    up_proj = jnp.dot(row_block, up_cols, preferred_element_type=jnp.float32)
    d_hidden = lax.dot_general(row_grads, down_rows, contract, preferred_element_type=jnp.float32)
    sigmoid_gate = jax.nn.sigmoid(gate_proj)
    d_gate = (d_hidden * up_proj * sigmoid_gate * (1.0 + gate_proj * (1.0 - sigmoid_gate))).astype(jnp.bfloat16)
    d_up = (d_hidden * gate_proj * sigmoid_gate).astype(jnp.bfloat16)
    running = jnp.zeros((row_block.shape[0], D), jnp.float32)
    for unit_block in range(SPAN):
        first_unit = unit_block * FF_DEV
        last_unit = first_unit + FF_DEV
        partial_sum = lax.dot_general(d_gate[:, first_unit:last_unit], gate_cols[:, first_unit:last_unit], contract, preferred_element_type=jnp.float32)
        partial_sum = partial_sum + lax.dot_general(d_up[:, first_unit:last_unit], up_cols[:, first_unit:last_unit], contract, preferred_element_type=jnp.float32)
        running = running + partial_sum.astype(jnp.bfloat16).astype(jnp.float32)
    return running.astype(jnp.bfloat16)


def split_experts(w_gate, w_up, w_down):
    gate_each = w_gate.reshape(D, EXPERTS, FF).transpose(1, 0, 2)
    up_each = w_up.reshape(D, EXPERTS, FF).transpose(1, 0, 2)
    down_each = w_down.reshape(EXPERTS, FF, D)
    return gate_each, up_each, down_each


def with_zero_row(tokens):
    return jnp.concatenate([tokens, jnp.zeros((1, D), tokens.dtype)], axis=0)


def section_forward(tokens, chosen, router, w_gate, w_up, w_down):
    slot_index, slot_table = slots_of(chosen)
    weight = routing_weight(tokens, router, chosen)
    padded = with_zero_row(tokens)
    gate_each, up_each, down_each = split_experts(w_gate, w_up, w_down)

    def per_expert(inputs):
        slot_row, gate_cols, up_cols, down_rows = inputs
        return expert_forward(padded[slot_row], gate_cols, up_cols, down_rows)

    outputs = lax.map(per_expert, (slot_table, gate_each, up_each, down_each))
    expert_out = lax.optimization_barrier(outputs[chosen, slot_index]).astype(jnp.float32)
    return (tokens.astype(jnp.float32) + weight[:, None] * expert_out).astype(jnp.bfloat16)


def section_backward(saved, chosen, grads, router, w_gate, w_up, w_down):
    slot_index, slot_table = slots_of(chosen)
    weight = routing_weight(saved, router, chosen)
    weighted = (weight[:, None] * grads.astype(jnp.float32)).astype(jnp.bfloat16)
    padded = with_zero_row(saved)
    padded_grads = with_zero_row(weighted)
    gate_each, up_each, down_each = split_experts(w_gate, w_up, w_down)

    def per_expert(inputs):
        slot_row, gate_cols, up_cols, down_rows = inputs
        return expert_backward(padded[slot_row], padded_grads[slot_row], gate_cols, up_cols, down_rows)

    outputs = lax.map(per_expert, (slot_table, gate_each, up_each, down_each))
    expert_out = lax.optimization_barrier(outputs[chosen, slot_index]).astype(jnp.float32)
    return (grads.astype(jnp.float32) + expert_out).astype(jnp.bfloat16)


def reference(fwd_in, fwd_ids, saved_in, bwd_ids, grad_in, router, w_gate, w_up, w_down):
    forward_list = []
    backward_list = []
    for section_index in range(N_PP):
        forward_list.append(section_forward(fwd_in[section_index], fwd_ids[section_index, :, 0], router[section_index], w_gate[section_index], w_up[section_index], w_down[section_index]))
        backward_list.append(section_backward(saved_in[section_index], bwd_ids[section_index, :, 0], grad_in[section_index], router[section_index], w_gate[section_index], w_up[section_index], w_down[section_index]))
    fwd_next = jnp.roll(jnp.stack(forward_list), 1, axis=0)
    grad_next = jnp.roll(jnp.stack(backward_list), -1, axis=0)
    return fwd_next, grad_next
```

```python
import functools

import jax
import jax.numpy as jnp
from jax import lax
from jax.experimental import pallas as pl
from jax.experimental.pallas import tpu as pltpu
from jax.sharding import PartitionSpec as P

route_scale = 2.5
contract = (((1,), (1,)), ((), ()))


def shortened(value):

    def short(part):
        return part.astype(jnp.bfloat16) if part.dtype == jnp.float32 else part

    return jax.tree.map(short, value)


def swapped(value, axis, distance):
    return lax.ppermute(value, axis, [(i, i ^ 1 << distance) for i in range(lax.axis_size(axis))])


def from_behind(value, axis, steps):
    count = lax.axis_size(axis)
    pairs = [(source, (source + steps) % count) for source in range(count)]
    return lax.ppermute(value, axis, pairs)


def order_slots(chosen, experts, capacity):
    token_count = chosen.shape[0]
    onehot = (chosen[:, None] == jnp.arange(experts, dtype=jnp.int32)[None, :]).astype(jnp.int32)
    before = jnp.cumsum(onehot, axis=0) - onehot
    ranking = jnp.sum(before * onehot, axis=1)
    slot_table = jnp.full((experts * capacity,), token_count, jnp.int32)
    slot_table = slot_table.at[chosen * capacity + ranking].set(
        jnp.arange(token_count, dtype=jnp.int32)
    )
    return (onehot, ranking, slot_table)


def routing_weight(tokens, router, onehot):
    logits = jnp.dot(tokens.astype(jnp.float32), router, precision=lax.Precision.HIGHEST)
    picked = jnp.sum(jnp.where(onehot > 0, logits, 0.0), axis=1)
    return route_scale * jax.nn.sigmoid(picked)


def with_zero_row(tokens):
    return jnp.concatenate([tokens, jnp.zeros((1, tokens.shape[1]), tokens.dtype)], axis=0)


def expert_forward(row_block, gate_cols, up_cols, down_rows):
    gate_proj = jnp.dot(row_block, gate_cols, preferred_element_type=jnp.float32)
    up_proj = jnp.dot(row_block, up_cols, preferred_element_type=jnp.float32)
    hidden = (gate_proj * jax.nn.sigmoid(gate_proj) * up_proj).astype(jnp.bfloat16)
    return jnp.dot(hidden, down_rows, preferred_element_type=jnp.float32).astype(jnp.bfloat16)


def expert_backward(row_block, row_grads, joined_cols, down_rows):
    unit_count = down_rows.shape[0]
    both_proj = jnp.dot(row_block, joined_cols, preferred_element_type=jnp.float32)
    gate_proj = both_proj[:, :unit_count]
    up_proj = both_proj[:, unit_count:]
    d_hidden = lax.dot_general(row_grads, down_rows, contract, preferred_element_type=jnp.float32)
    sigmoid_gate = jax.nn.sigmoid(gate_proj)
    d_gate = (d_hidden * up_proj * sigmoid_gate * (1.0 + gate_proj * (1.0 - sigmoid_gate))).astype(
        jnp.bfloat16
    )
    d_up = (d_hidden * gate_proj * sigmoid_gate).astype(jnp.bfloat16)
    d_joined = jnp.concatenate([d_gate, d_up], axis=1)
    partial_sum = lax.dot_general(
        d_joined, joined_cols, contract, preferred_element_type=jnp.float32
    )
    return partial_sum.astype(jnp.bfloat16)


def arrange(own_rows, peer_rows, own_bit):
    return jnp.where(
        own_bit == 0, jnp.stack([own_rows, peer_rows]), jnp.stack([peer_rows, own_rows])
    )


def per_device(fwd_in, fwd_ids, saved_in, bwd_ids, grad_in, router, w_gate, w_up, w_down):
    experts = router.shape[-1]
    owners = lax.axis_size("ep")
    group_size = owners // experts
    bit_count = group_size.bit_length() - 1
    own_index = lax.axis_index("ep")
    token_count = fwd_in.shape[1]
    width = fwd_in.shape[2]
    capacity = group_size * max(1, 5 * token_count // (4 * experts * group_size))
    quarter_slots = capacity // group_size
    router_section = router[0]
    gate_cols = w_gate[0]
    up_cols = w_up[0]
    down_rows = w_down[0]
    joined_cols = jnp.concatenate([gate_cols, up_cols], axis=1)
    fwd_tokens = fwd_in[0]
    fwd_chosen = fwd_ids[0, :, 0]
    fwd_onehot, fwd_rank, fwd_table = order_slots(fwd_chosen, experts, capacity)
    fwd_weight = routing_weight(fwd_tokens, router_section, fwd_onehot)
    fwd_padded = with_zero_row(fwd_tokens)
    saved_tokens = saved_in[0]
    bwd_chosen = bwd_ids[0, :, 0]
    grad_tokens = grad_in[0]
    bwd_onehot, bwd_rank, bwd_table = order_slots(bwd_chosen, experts, capacity)
    bwd_weight = routing_weight(saved_tokens, router_section, bwd_onehot)
    weighted = (bwd_weight[:, None] * grad_tokens.astype(jnp.float32)).astype(jnp.bfloat16)
    saved_padded = with_zero_row(saved_tokens)
    weighted_padded = with_zero_row(weighted)
    fwd_index = (
        fwd_table.reshape(experts, quarter_slots, group_size)
        .transpose(0, 2, 1)
        .reshape(owners, quarter_slots)
    )
    gathered = lax.all_to_all(
        jnp.take(fwd_padded, fwd_index, axis=0), "ep", split_axis=0, concat_axis=0, tiled=True
    )
    for bit_number in range(bit_count):
        own_bit = own_index >> bit_number & 1
        peer_rows = swapped(shortened(gathered), "ep", bit_number).astype(gathered.dtype)
        gathered = arrange(gathered, peer_rows, own_bit)
    partial_out = expert_forward(gathered.reshape(-1, width), gate_cols, up_cols, down_rows)
    partial_out = partial_out.reshape(group_size, 1, owners * quarter_slots, width)
    for bit_number in reversed(range(bit_count)):
        own_bit = own_index >> bit_number & 1
        half_rows = partial_out.shape[0] // 2
        kept_half = lax.dynamic_slice_in_dim(partial_out, own_bit * half_rows, half_rows, 0)
        sent_half = lax.dynamic_slice_in_dim(partial_out, (1 - own_bit) * half_rows, half_rows, 0)
        partial_out = jnp.concatenate([kept_half, swapped(sent_half, "ep", bit_number)], axis=1)
    summed = jnp.sum(partial_out, axis=(0, 1), dtype=jnp.float32).astype(jnp.bfloat16)
    returned = lax.all_to_all(
        summed.reshape(owners, quarter_slots, width), "ep", split_axis=0, concat_axis=0, tiled=True
    ).reshape(-1, width)
    source_slot = (
        fwd_chosen * group_size + fwd_rank % group_size
    ) * quarter_slots + fwd_rank // group_size
    fwd_expert = jnp.take(returned, source_slot, axis=0).astype(jnp.float32)
    bwd_index = (
        bwd_table.reshape(experts, quarter_slots, group_size)
        .transpose(0, 2, 1)
        .reshape(owners, quarter_slots)
    )
    saved_rows, grad_rows = (
        lax.all_to_all(
            jnp.take(saved_padded, bwd_index, axis=0), "ep", split_axis=0, concat_axis=0, tiled=True
        ),
        lax.all_to_all(
            jnp.take(weighted_padded, bwd_index, axis=0),
            "ep",
            split_axis=0,
            concat_axis=0,
            tiled=True,
        ),
    )
    for bit_number in range(bit_count):
        own_bit = own_index >> bit_number & 1
        peer_saved, peer_grads = (
            swapped(shortened(saved_rows), "ep", bit_number).astype(saved_rows.dtype),
            swapped(shortened(grad_rows), "ep", bit_number).astype(grad_rows.dtype),
        )
        saved_rows = arrange(saved_rows, peer_saved, own_bit)
        grad_rows = arrange(grad_rows, peer_grads, own_bit)
    partial_grad = expert_backward(
        saved_rows.reshape(-1, width), grad_rows.reshape(-1, width), joined_cols, down_rows
    )
    partial_grad = partial_grad.reshape(group_size, 1, owners * quarter_slots, width)
    for bit_number in reversed(range(bit_count)):
        own_bit = own_index >> bit_number & 1
        half_rows = partial_grad.shape[0] // 2
        kept_half = lax.dynamic_slice_in_dim(partial_grad, own_bit * half_rows, half_rows, 0)
        sent_half = lax.dynamic_slice_in_dim(partial_grad, (1 - own_bit) * half_rows, half_rows, 0)
        partial_grad = jnp.concatenate([kept_half, swapped(sent_half, "ep", bit_number)], axis=1)
    summed_grad = jnp.sum(partial_grad, axis=(0, 1), dtype=jnp.float32).astype(jnp.bfloat16)
    returned_grad = lax.all_to_all(
        summed_grad.reshape(owners, quarter_slots, width),
        "ep",
        split_axis=0,
        concat_axis=0,
        tiled=True,
    ).reshape(-1, width)
    grad_slot = (
        bwd_chosen * group_size + bwd_rank % group_size
    ) * quarter_slots + bwd_rank // group_size
    bwd_expert = jnp.take(returned_grad, grad_slot, axis=0).astype(jnp.float32)
    fwd_section = (fwd_tokens.astype(jnp.float32) + fwd_weight[:, None] * fwd_expert).astype(
        jnp.bfloat16
    )
    grad_section = (grad_tokens.astype(jnp.float32) + bwd_expert).astype(jnp.bfloat16)
    fwd_next = from_behind(fwd_section[None], "pp", 1)
    grad_next = from_behind(grad_section[None], "pp", -1)
    return (fwd_next, grad_next)


BASE_ROWS = 16
CUTS = 4
ROWS_BYTES = 2


def transposed_dot(left, right):
    return lax.dot_general(left, right, contract, preferred_element_type=jnp.float32)


def plain_dot(left, right):
    return jnp.dot(left, right, preferred_element_type=jnp.float32)


def slot_masks(ids_row, me, experts):
    tokens = ids_row.shape[1]
    wanted = lax.broadcasted_iota(jnp.int32, (experts, tokens), 0) == ids_row
    chosen = jnp.where(wanted, 1.0, 0.0)
    earlier = jnp.where(
        lax.broadcasted_iota(jnp.int32, (tokens, tokens), 0)
        < lax.broadcasted_iota(jnp.int32, (tokens, tokens), 1),
        1.0,
        0.0,
    )
    before = plain_dot(chosen.astype(jnp.bfloat16), earlier.astype(jnp.bfloat16))
    rank = jnp.sum(before * chosen, axis=0, keepdims=True).astype(jnp.int32)
    row = lax.broadcasted_iota(jnp.int32, (experts * BASE_ROWS, tokens), 0)
    mine = ids_row == ((row // BASE_ROWS) ^ me)
    place = row % BASE_ROWS
    base = jnp.where(mine & (rank == place), 1.0, 0.0).astype(jnp.bfloat16)
    extra = mine & (rank == BASE_ROWS + place % CUTS)
    pieces = [
        jnp.where(extra & (place // CUTS == q), 1.0, 0.0).astype(jnp.bfloat16) for q in range(CUTS)
    ]
    return base, pieces


def pack_kernel(experts, ids_ref, x_ref, *out_refs):
    me = lax.axis_index("ep")
    width = x_ref.shape[1]
    piece = width // CUTS
    base, pieces = slot_masks(ids_ref[...], me, experts)
    for q in range(CUTS):
        columns = slice(q * piece, (q + 1) * piece)
        packed = plain_dot(base, x_ref[:, columns]).astype(jnp.bfloat16)
        for k in range(experts):
            out_refs[k][:, columns] = packed[k * BASE_ROWS : (k + 1) * BASE_ROWS]
    extra = plain_dot(pieces[0], x_ref[:, :piece])
    for q in range(1, CUTS):
        extra = extra + plain_dot(pieces[q], x_ref[:, q * piece : (q + 1) * piece])
    extra = extra.astype(jnp.bfloat16)
    for k in range(experts):
        out_refs[k][:, width:] = extra[k * BASE_ROWS : (k + 1) * BASE_ROWS]


def unpack_kernel(experts, ids_ref, *refs):
    me = lax.axis_index("ep")
    message_refs, out_ref = refs[:experts], refs[experts]
    width = out_ref.shape[1]
    piece = width // CUTS
    base, pieces = slot_masks(ids_ref[...], me, experts)
    from_rows = (((0,), (0,)), ((), ()))
    extra = jnp.concatenate([ref[:, width:] for ref in message_refs], axis=0)
    for q in range(CUTS):
        columns = slice(q * piece, (q + 1) * piece)
        rows = jnp.concatenate([ref[:, columns] for ref in message_refs], axis=0)
        total = lax.dot_general(base, rows, from_rows, preferred_element_type=jnp.float32)
        total = total + lax.dot_general(
            pieces[q], extra, from_rows, preferred_element_type=jnp.float32
        )
        out_ref[:, columns] = total.astype(jnp.bfloat16)


def piece_places(experts, q):
    shape = (experts * CUTS, experts * BASE_ROWS)
    slot = lax.broadcasted_iota(jnp.int32, shape, 0)
    row = lax.broadcasted_iota(jnp.int32, shape, 1)
    same = (slot // CUTS == row // BASE_ROWS) & (row % BASE_ROWS == q * CUTS + slot % CUTS)
    return jnp.where(same, 1.0, 0.0).astype(jnp.bfloat16)


def spread(message_refs, rows_ref):
    experts = len(message_refs)
    width = rows_ref.shape[1]
    piece = width // CUTS
    first = experts * BASE_ROWS
    for k, ref in enumerate(message_refs):
        rows_ref[k * BASE_ROWS : (k + 1) * BASE_ROWS, :] = ref[:, :width]
    extra = jnp.concatenate([ref[:, width:] for ref in message_refs], axis=0)
    for q in range(CUTS):
        picked = plain_dot(piece_places(experts, q), extra)
        rows_ref[first:, q * piece : (q + 1) * piece] = picked.astype(jnp.bfloat16)


def collect(rows_ref, message_refs):
    experts = len(message_refs)
    width = rows_ref.shape[1]
    piece = width // CUTS
    first = experts * BASE_ROWS
    from_rows = (((0,), (0,)), ((), ()))
    extra = 0.0
    for q in range(CUTS):
        extra = extra + lax.dot_general(
            piece_places(experts, q),
            rows_ref[first:, q * piece : (q + 1) * piece],
            from_rows,
            preferred_element_type=jnp.float32,
        )
    extra = extra.astype(jnp.bfloat16)
    for k, ref in enumerate(message_refs):
        ref[:, :width] = rows_ref[k * BASE_ROWS : (k + 1) * BASE_ROWS, :]
        ref[:, width:] = extra[k * BASE_ROWS : (k + 1) * BASE_ROWS]


def row_weight(rows_ref, router_ref):
    me = lax.axis_index("ep")
    centroid = router_ref[pl.ds(me, 1), :]
    logits = jnp.sum(rows_ref[...].astype(jnp.float32) * centroid, axis=1, keepdims=True)
    return route_scale * jax.nn.sigmoid(logits)


def forward_kernel(experts, router_ref, gate_ref, up_ref, down_ref, *refs):
    message_refs, out_refs = refs[:experts], refs[experts : 2 * experts]
    rows_ref, total_ref = refs[2 * experts :]
    step = pl.program_id(0)

    @pl.when(step == 0)
    def _():
        spread(message_refs, rows_ref)

    rows = rows_ref[...]
    gate_proj = plain_dot(rows, gate_ref[...])
    up_proj = plain_dot(rows, up_ref[...])
    hidden = (gate_proj * jax.nn.sigmoid(gate_proj) * up_proj).astype(jnp.bfloat16)
    part = plain_dot(hidden, down_ref[...])

    @pl.when(step == 0)
    def _():
        total_ref[...] = part

    @pl.when(step > 0)
    def _():
        total_ref[...] += part

    @pl.when(step == pl.num_programs(0) - 1)
    def _():
        weight = row_weight(rows_ref, router_ref)
        expert = total_ref[...].astype(jnp.bfloat16).astype(jnp.float32)
        section = rows_ref[...].astype(jnp.float32) + weight * expert
        rows_ref[...] = section.astype(jnp.bfloat16)
        collect(rows_ref, out_refs)


def backward_kernel(experts, router_ref, gate_ref, up_ref, down_ref, *refs):
    saved_refs, grad_refs = refs[:experts], refs[experts : 2 * experts]
    out_refs = refs[2 * experts : 3 * experts]
    rows_ref, grads_ref, weighted_ref, total_ref = refs[3 * experts :]
    step = pl.program_id(0)

    @pl.when(step == 0)
    def _():
        spread(saved_refs, rows_ref)
        spread(grad_refs, grads_ref)
        weight = row_weight(rows_ref, router_ref)
        weighted = weight * grads_ref[...].astype(jnp.float32)
        weighted_ref[...] = weighted.astype(jnp.bfloat16)

    rows = rows_ref[...]
    gate_proj = plain_dot(rows, gate_ref[...])
    up_proj = plain_dot(rows, up_ref[...])
    d_hidden = transposed_dot(weighted_ref[...], down_ref[...])
    sigmoid_gate = jax.nn.sigmoid(gate_proj)
    d_gate = d_hidden * up_proj * sigmoid_gate * (1.0 + gate_proj * (1.0 - sigmoid_gate))
    d_up = d_hidden * gate_proj * sigmoid_gate
    part = transposed_dot(d_gate.astype(jnp.bfloat16), gate_ref[...])
    part = part + transposed_dot(d_up.astype(jnp.bfloat16), up_ref[...])

    @pl.when(step == 0)
    def _():
        total_ref[...] = part

    @pl.when(step > 0)
    def _():
        total_ref[...] += part

    @pl.when(step == pl.num_programs(0) - 1)
    def _():
        expert = total_ref[...].astype(jnp.bfloat16).astype(jnp.float32)
        section = grads_ref[...].astype(jnp.float32) + expert
        rows_ref[...] = section.astype(jnp.bfloat16)
        collect(rows_ref, out_refs)


def pack(ids_row, rows, experts):
    tokens, width = rows.shape
    shape = jax.ShapeDtypeStruct((BASE_ROWS, width + width // CUTS), rows.dtype)
    slots = experts * BASE_ROWS
    return pl.pallas_call(
        functools.partial(pack_kernel, experts),
        out_shape=[shape] * experts,
        compiler_params=pltpu.CompilerParams(vmem_limit_bytes=16 << 20),
        cost_estimate=pl.CostEstimate(
            flops=4 * slots * tokens * width,
            bytes_accessed=2 * ROWS_BYTES * slots * width,
            transcendentals=0,
        ),
        name="pack",
    )(ids_row, rows)


def unpack(ids_row, messages, experts):
    tokens = ids_row.shape[1]
    width = messages[0].shape[1] * CUTS // (CUTS + 1)
    slots = experts * BASE_ROWS
    return pl.pallas_call(
        functools.partial(unpack_kernel, experts),
        out_shape=jax.ShapeDtypeStruct((tokens, width), messages[0].dtype),
        compiler_params=pltpu.CompilerParams(vmem_limit_bytes=16 << 20),
        cost_estimate=pl.CostEstimate(
            flops=4 * slots * tokens * width,
            bytes_accessed=2 * ROWS_BYTES * slots * width,
            transcendentals=0,
        ),
        name="unpack",
    )(ids_row, *messages)


def expert_call(kernel, name, router_rows, gate_cols, up_cols, down_rows, messages, experts, products):
    width, units = gate_cols.shape
    row_count = experts * (BASE_ROWS + CUTS)
    steps = 4 if units % 512 == 0 else 1
    part = units // steps
    message_shape = messages[0].shape
    whole = pl.BlockSpec(message_shape, lambda j: (0, 0))
    extra_scratch = 2 if len(messages) > experts else 0
    return pl.pallas_call(
        functools.partial(kernel, experts),
        grid=(steps,),
        in_specs=[
            pl.BlockSpec(router_rows.shape, lambda j: (0, 0)),
            pl.BlockSpec((width, part), lambda j: (0, j)),
            pl.BlockSpec((width, part), lambda j: (0, j)),
            pl.BlockSpec((part, width), lambda j: (j, 0)),
        ]
        + [whole] * len(messages),
        out_specs=[whole] * experts,
        out_shape=[jax.ShapeDtypeStruct(message_shape, messages[0].dtype)] * experts,
        scratch_shapes=[pltpu.VMEM((row_count, width), jnp.bfloat16)] * (1 + extra_scratch)
        + [pltpu.VMEM((row_count, width), jnp.float32)],
        compiler_params=pltpu.CompilerParams(vmem_limit_bytes=40 << 20),
        cost_estimate=pl.CostEstimate(
            flops=2 * products * row_count * width * units,
            bytes_accessed=3 * ROWS_BYTES * width * units,
            transcendentals=row_count * units,
        ),
        name=name,
    )(router_rows, gate_cols, up_cols, down_rows, *messages)


def exchanged(messages, experts):
    return [messages[0]] + [
        lax.ppermute(messages[k], "ep", [(i, i ^ k) for i in range(experts)])
        for k in range(1, experts)
    ]


def returned(messages, experts, steps):
    sections = lax.axis_size("pp")
    back = []
    for k in range(experts):
        pairs = [
            (p * experts + e, (p + steps) % sections * experts + (e ^ k))
            for p in range(sections)
            for e in range(experts)
        ]
        back.append(lax.ppermute(messages[k], ("pp", "ep"), pairs))
    return back


def per_device_whole(fwd_in, fwd_ids, saved_in, bwd_ids, grad_in, router, w_gate, w_up, w_down):
    experts = router.shape[-1]
    token_count = fwd_in.shape[1]
    router_rows = router[0].T
    weights = (w_gate[0], w_up[0], w_down[0])
    fwd_row = fwd_ids.reshape(1, token_count)
    bwd_row = bwd_ids.reshape(1, token_count)
    fwd_rows = exchanged(pack(fwd_row, fwd_in[0], experts), experts)
    saved_rows = exchanged(pack(bwd_row, saved_in[0], experts), experts)
    grad_rows = exchanged(pack(bwd_row, grad_in[0], experts), experts)
    fwd_row_next = from_behind(fwd_row, "pp", 1)
    bwd_row_next = from_behind(bwd_row, "pp", -1)
    fwd_out = expert_call(forward_kernel, "forward", router_rows, *weights, fwd_rows, experts, 3)
    fwd_back = returned(fwd_out, experts, 1)
    bwd_out = expert_call(
        backward_kernel, "backward", router_rows, *weights, saved_rows + grad_rows, experts, 5
    )
    bwd_back = returned(bwd_out, experts, -1)
    fwd_next = unpack(fwd_row_next, fwd_back, experts)
    grad_next = unpack(bwd_row_next, bwd_back, experts)
    return (fwd_next[None], grad_next[None])


def solution(mesh):
    in_specs = (
        P("pp", "ep", None),
        P("pp", "ep", None),
        P("pp", "ep", None),
        P("pp", "ep", None),
        P("pp", "ep", None),
        P("pp", None, None),
        P("pp", None, "ep"),
        P("pp", None, "ep"),
        P("pp", "ep", None),
    )
    out_specs = (P("pp", "ep", None), P("pp", "ep", None))

    def layer(*arrays):
        token_count = arrays[0].shape[1] // mesh.shape["ep"]
        width = arrays[0].shape[2]
        experts = arrays[5].shape[-1]
        whole = (
            mesh.shape["ep"] == experts
            and experts & (experts - 1) == 0
            and 5 * token_count // (4 * experts) == BASE_ROWS + CUTS
            and width % (128 * CUTS) == 0
        )
        return jax.shard_map(
            per_device_whole if whole else per_device,
            mesh=mesh,
            in_specs=in_specs,
            out_specs=out_specs,
            check_vma=False,
        )(*arrays)

    return layer
```

```python
import functools

import jax
import jax.numpy as jnp
from jax import lax
from jax.experimental import pallas as pl
from jax.experimental.pallas import tpu as pltpu
from jax.sharding import PartitionSpec as P

route_scale = 2.5
contract = (((1,), (1,)), ((), ()))


def shortened(value):

    def short(part):
        return part.astype(jnp.bfloat16) if part.dtype == jnp.float32 else part

    return jax.tree.map(short, value)


def swapped(value, axis, distance):
    return lax.ppermute(value, axis, [(i, i ^ 1 << distance) for i in range(lax.axis_size(axis))])


def from_behind(value, axis, steps):
    count = lax.axis_size(axis)
    pairs = [(source, (source + steps) % count) for source in range(count)]
    return lax.ppermute(value, axis, pairs)


def order_slots(chosen, experts, capacity):
    token_count = chosen.shape[0]
    onehot = (chosen[:, None] == jnp.arange(experts, dtype=jnp.int32)[None, :]).astype(jnp.int32)
    before = jnp.cumsum(onehot, axis=0) - onehot
    ranking = jnp.sum(before * onehot, axis=1)
    slot_table = jnp.full((experts * capacity,), token_count, jnp.int32)
    slot_table = slot_table.at[chosen * capacity + ranking].set(
        jnp.arange(token_count, dtype=jnp.int32)
    )
    return (onehot, ranking, slot_table)


def routing_weight(tokens, router, onehot):
    logits = jnp.dot(tokens.astype(jnp.float32), router, precision=lax.Precision.HIGHEST)
    picked = jnp.sum(jnp.where(onehot > 0, logits, 0.0), axis=1)
    return route_scale * jax.nn.sigmoid(picked)


def with_zero_row(tokens):
    return jnp.concatenate([tokens, jnp.zeros((1, tokens.shape[1]), tokens.dtype)], axis=0)


def expert_forward(row_block, gate_cols, up_cols, down_rows):
    gate_proj = jnp.dot(row_block, gate_cols, preferred_element_type=jnp.float32)
    up_proj = jnp.dot(row_block, up_cols, preferred_element_type=jnp.float32)
    hidden = (gate_proj * jax.nn.sigmoid(gate_proj) * up_proj).astype(jnp.bfloat16)
    return jnp.dot(hidden, down_rows, preferred_element_type=jnp.float32).astype(jnp.bfloat16)


def expert_backward(row_block, row_grads, joined_cols, down_rows):
    unit_count = down_rows.shape[0]
    both_proj = jnp.dot(row_block, joined_cols, preferred_element_type=jnp.float32)
    gate_proj = both_proj[:, :unit_count]
    up_proj = both_proj[:, unit_count:]
    d_hidden = lax.dot_general(row_grads, down_rows, contract, preferred_element_type=jnp.float32)
    sigmoid_gate = jax.nn.sigmoid(gate_proj)
    d_gate = (d_hidden * up_proj * sigmoid_gate * (1.0 + gate_proj * (1.0 - sigmoid_gate))).astype(
        jnp.bfloat16
    )
    d_up = (d_hidden * gate_proj * sigmoid_gate).astype(jnp.bfloat16)
    d_joined = jnp.concatenate([d_gate, d_up], axis=1)
    partial_sum = lax.dot_general(
        d_joined, joined_cols, contract, preferred_element_type=jnp.float32
    )
    return partial_sum.astype(jnp.bfloat16)


def arrange(own_rows, peer_rows, own_bit):
    return jnp.where(
        own_bit == 0, jnp.stack([own_rows, peer_rows]), jnp.stack([peer_rows, own_rows])
    )


def per_device(fwd_in, fwd_ids, saved_in, bwd_ids, grad_in, router, w_gate, w_up, w_down):
    experts = router.shape[-1]
    owners = lax.axis_size("ep")
    group_size = owners // experts
    bit_count = group_size.bit_length() - 1
    own_index = lax.axis_index("ep")
    token_count = fwd_in.shape[1]
    width = fwd_in.shape[2]
    capacity = group_size * max(1, 5 * token_count // (4 * experts * group_size))
    quarter_slots = capacity // group_size
    router_section = router[0]
    gate_cols = w_gate[0]
    up_cols = w_up[0]
    down_rows = w_down[0]
    joined_cols = jnp.concatenate([gate_cols, up_cols], axis=1)
    fwd_tokens = fwd_in[0]
    fwd_chosen = fwd_ids[0, :, 0]
    fwd_onehot, fwd_rank, fwd_table = order_slots(fwd_chosen, experts, capacity)
    fwd_weight = routing_weight(fwd_tokens, router_section, fwd_onehot)
    fwd_padded = with_zero_row(fwd_tokens)
    saved_tokens = saved_in[0]
    bwd_chosen = bwd_ids[0, :, 0]
    grad_tokens = grad_in[0]
    bwd_onehot, bwd_rank, bwd_table = order_slots(bwd_chosen, experts, capacity)
    bwd_weight = routing_weight(saved_tokens, router_section, bwd_onehot)
    weighted = (bwd_weight[:, None] * grad_tokens.astype(jnp.float32)).astype(jnp.bfloat16)
    saved_padded = with_zero_row(saved_tokens)
    weighted_padded = with_zero_row(weighted)
    fwd_index = (
        fwd_table.reshape(experts, quarter_slots, group_size)
        .transpose(0, 2, 1)
        .reshape(owners, quarter_slots)
    )
    gathered = lax.all_to_all(
        jnp.take(fwd_padded, fwd_index, axis=0), "ep", split_axis=0, concat_axis=0, tiled=True
    )
    for bit_number in range(bit_count):
        own_bit = own_index >> bit_number & 1
        peer_rows = swapped(shortened(gathered), "ep", bit_number).astype(gathered.dtype)
        gathered = arrange(gathered, peer_rows, own_bit)
    partial_out = expert_forward(gathered.reshape(-1, width), gate_cols, up_cols, down_rows)
    partial_out = partial_out.reshape(group_size, 1, owners * quarter_slots, width)
    for bit_number in reversed(range(bit_count)):
        own_bit = own_index >> bit_number & 1
        half_rows = partial_out.shape[0] // 2
        kept_half = lax.dynamic_slice_in_dim(partial_out, own_bit * half_rows, half_rows, 0)
        sent_half = lax.dynamic_slice_in_dim(partial_out, (1 - own_bit) * half_rows, half_rows, 0)
        partial_out = jnp.concatenate([kept_half, swapped(sent_half, "ep", bit_number)], axis=1)
    summed = jnp.sum(partial_out, axis=(0, 1), dtype=jnp.float32).astype(jnp.bfloat16)
    returned = lax.all_to_all(
        summed.reshape(owners, quarter_slots, width), "ep", split_axis=0, concat_axis=0, tiled=True
    ).reshape(-1, width)
    source_slot = (
        fwd_chosen * group_size + fwd_rank % group_size
    ) * quarter_slots + fwd_rank // group_size
    fwd_expert = jnp.take(returned, source_slot, axis=0).astype(jnp.float32)
    bwd_index = (
        bwd_table.reshape(experts, quarter_slots, group_size)
        .transpose(0, 2, 1)
        .reshape(owners, quarter_slots)
    )
    saved_rows, grad_rows = (
        lax.all_to_all(
            jnp.take(saved_padded, bwd_index, axis=0), "ep", split_axis=0, concat_axis=0, tiled=True
        ),
        lax.all_to_all(
            jnp.take(weighted_padded, bwd_index, axis=0),
            "ep",
            split_axis=0,
            concat_axis=0,
            tiled=True,
        ),
    )
    for bit_number in range(bit_count):
        own_bit = own_index >> bit_number & 1
        peer_saved, peer_grads = (
            swapped(shortened(saved_rows), "ep", bit_number).astype(saved_rows.dtype),
            swapped(shortened(grad_rows), "ep", bit_number).astype(grad_rows.dtype),
        )
        saved_rows = arrange(saved_rows, peer_saved, own_bit)
        grad_rows = arrange(grad_rows, peer_grads, own_bit)
    partial_grad = expert_backward(
        saved_rows.reshape(-1, width), grad_rows.reshape(-1, width), joined_cols, down_rows
    )
    partial_grad = partial_grad.reshape(group_size, 1, owners * quarter_slots, width)
    for bit_number in reversed(range(bit_count)):
        own_bit = own_index >> bit_number & 1
        half_rows = partial_grad.shape[0] // 2
        kept_half = lax.dynamic_slice_in_dim(partial_grad, own_bit * half_rows, half_rows, 0)
        sent_half = lax.dynamic_slice_in_dim(partial_grad, (1 - own_bit) * half_rows, half_rows, 0)
        partial_grad = jnp.concatenate([kept_half, swapped(sent_half, "ep", bit_number)], axis=1)
    summed_grad = jnp.sum(partial_grad, axis=(0, 1), dtype=jnp.float32).astype(jnp.bfloat16)
    returned_grad = lax.all_to_all(
        summed_grad.reshape(owners, quarter_slots, width),
        "ep",
        split_axis=0,
        concat_axis=0,
        tiled=True,
    ).reshape(-1, width)
    grad_slot = (
        bwd_chosen * group_size + bwd_rank % group_size
    ) * quarter_slots + bwd_rank // group_size
    bwd_expert = jnp.take(returned_grad, grad_slot, axis=0).astype(jnp.float32)
    fwd_section = (fwd_tokens.astype(jnp.float32) + fwd_weight[:, None] * fwd_expert).astype(
        jnp.bfloat16
    )
    grad_section = (grad_tokens.astype(jnp.float32) + bwd_expert).astype(jnp.bfloat16)
    fwd_next = from_behind(fwd_section[None], "pp", 1)
    grad_next = from_behind(grad_section[None], "pp", -1)
    return (fwd_next, grad_next)


BASE_ROWS = 16
CUTS = 4
ROWS_BYTES = 2
VMEM_BYTES = 44 << 20


def transposed_dot(left, right):
    return lax.dot_general(left, right, contract, preferred_element_type=jnp.float32)


def plain_dot(left, right):
    return jnp.dot(left, right, preferred_element_type=jnp.float32)


def slot_masks(ids_row, me, experts):
    tokens = ids_row.shape[1]
    wanted = lax.broadcasted_iota(jnp.int32, (experts, tokens), 0) == ids_row
    chosen = jnp.where(wanted, 1.0, 0.0)
    earlier = jnp.where(
        lax.broadcasted_iota(jnp.int32, (tokens, tokens), 0)
        < lax.broadcasted_iota(jnp.int32, (tokens, tokens), 1),
        1.0,
        0.0,
    )
    before = plain_dot(chosen.astype(jnp.bfloat16), earlier.astype(jnp.bfloat16))
    rank = jnp.sum(before * chosen, axis=0, keepdims=True).astype(jnp.int32)
    row = lax.broadcasted_iota(jnp.int32, (experts * BASE_ROWS, tokens), 0)
    mine = ids_row == ((row // BASE_ROWS) ^ me)
    place = row % BASE_ROWS
    base = jnp.where(mine & (rank == place), 1.0, 0.0).astype(jnp.bfloat16)
    extra = mine & (rank == BASE_ROWS + place % CUTS)
    pieces = [
        jnp.where(extra & (place // CUTS == q), 1.0, 0.0).astype(jnp.bfloat16) for q in range(CUTS)
    ]
    return base, pieces


def pack_kernel(kind, joined, count, experts, ids_ref, *refs):
    x_refs = refs[:count]
    held_ref, made_ref, sems, out_sems = refs[-4:]
    copies = [pltpu.make_async_copy(x_refs[n], held_ref.at[n], sems.at[n]) for n in range(count)]
    for copy in copies:
        copy.start()
    width = held_ref.shape[2]
    piece = width // CUTS
    first = 0 if joined else lax.axis_index("ep")
    base, pieces = slot_masks(ids_ref[kind : kind + 1], first, experts)
    for n, copy in enumerate(copies):
        rows = slice(n * BASE_ROWS, (n + 1) * BASE_ROWS)
        copy.wait()
        extra = 0.0
        for q in range(CUTS):
            columns = slice(q * piece, (q + 1) * piece)
            part = held_ref[n, :, columns]
            packed = plain_dot(base, part).astype(jnp.bfloat16)
            extra = extra + plain_dot(pieces[q], part)
            for k in range(experts):
                made_ref[k, rows, columns] = packed[k * BASE_ROWS : (k + 1) * BASE_ROWS]
        extra = extra.astype(jnp.bfloat16)
        for k in range(experts):
            made_ref[k, rows, width:] = extra[k * BASE_ROWS : (k + 1) * BASE_ROWS]
    if joined:
        copies = [pltpu.make_async_copy(made_ref, refs[-5], out_sems.at[0])]
    else:
        out_refs = refs[-4 - experts : -4]
        copies = [
            pltpu.make_async_copy(made_ref.at[k], out_refs[k], out_sems.at[k]) for k in range(experts)
        ]
    for copy in copies:
        copy.start()
    for copy in copies:
        copy.wait()


def unpack_kernel(order, ids_ref, *refs):
    me = lax.axis_index("ep")
    experts = len(order)
    message_refs, out_ref = [refs[order.index(k)] for k in range(experts)], refs[experts]
    width = out_ref.shape[1]
    piece = width // CUTS
    base, pieces = slot_masks(ids_ref[...], me, experts)
    from_rows = (((0,), (0,)), ((), ()))
    extra = jnp.concatenate([ref[:, width:] for ref in message_refs], axis=0)
    for q in range(CUTS):
        columns = slice(q * piece, (q + 1) * piece)
        rows = jnp.concatenate([ref[:, columns] for ref in message_refs], axis=0)
        total = lax.dot_general(base, rows, from_rows, preferred_element_type=jnp.float32)
        total = total + lax.dot_general(
            pieces[q], extra, from_rows, preferred_element_type=jnp.float32
        )
        out_ref[:, columns] = total.astype(jnp.bfloat16)


def piece_places(experts, q):
    shape = (experts * CUTS, experts * BASE_ROWS)
    slot = lax.broadcasted_iota(jnp.int32, shape, 0)
    row = lax.broadcasted_iota(jnp.int32, shape, 1)
    same = (slot // CUTS == row // BASE_ROWS) & (row % BASE_ROWS == q * CUTS + slot % CUTS)
    return jnp.where(same, 1.0, 0.0).astype(jnp.bfloat16)


def message_copies(message_refs, place, rows_ref, extra_ref, sems):
    width = rows_ref.shape[1]
    taken = slice(place * BASE_ROWS, (place + 1) * BASE_ROWS)
    copies = []
    for k, ref in enumerate(message_refs):
        rows = slice(k * BASE_ROWS, (k + 1) * BASE_ROWS)
        parts = ((ref.at[taken, :width], rows_ref), (ref.at[taken, width:], extra_ref))
        for n, (source, target) in enumerate(parts):
            copies.append(pltpu.make_async_copy(source, target.at[rows, :], sems.at[n, k]))
    for copy in copies:
        copy.start()
    return copies


def spread(copies, rows_ref, extra_ref):
    width = rows_ref.shape[1]
    piece = width // CUTS
    experts = extra_ref.shape[0] // BASE_ROWS
    for copy in copies:
        copy.wait()
    for q in range(CUTS):
        picked = plain_dot(piece_places(experts, q), extra_ref[...])
        columns = slice(q * piece, (q + 1) * piece)
        rows_ref[experts * BASE_ROWS :, columns] = picked.astype(jnp.bfloat16)


def collect(rows_ref, extra_ref, message_refs, sems):
    experts = len(message_refs)
    width = rows_ref.shape[1]
    piece = width // CUTS
    first = experts * BASE_ROWS
    from_rows = (((0,), (0,)), ((), ()))
    extra = 0.0
    for q in range(CUTS):
        extra = extra + lax.dot_general(
            piece_places(experts, q),
            rows_ref[first:, q * piece : (q + 1) * piece],
            from_rows,
            preferred_element_type=jnp.float32,
        )
    extra_ref[...] = extra.astype(jnp.bfloat16)
    copies = []
    for k, ref in enumerate(message_refs):
        rows = slice(k * BASE_ROWS, (k + 1) * BASE_ROWS)
        parts = ((rows_ref, ref.at[:, :width]), (extra_ref, ref.at[:, width:]))
        for n, (source, target) in enumerate(parts):
            copies.append(pltpu.make_async_copy(source.at[rows, :], target, sems.at[n, k]))
    for copy in copies:
        copy.start()
    for copy in copies:
        copy.wait()


def row_weight(rows_ref, router_ref):
    me = lax.axis_index("ep")
    centroid = router_ref[pl.ds(me, 1), :]
    logits = jnp.sum(rows_ref[...].astype(jnp.float32) * centroid, axis=1, keepdims=True)
    return route_scale * jax.nn.sigmoid(logits)


def weight_copies(weight_refs, chunk_refs, sems):
    gate_ref, up_ref, down_ref = weight_refs
    steps, width, part = chunk_refs[0].shape
    copies = []
    for j in range(steps):
        units = slice(j * part, (j + 1) * part)
        sources = (gate_ref.at[:, units], up_ref.at[:, units], down_ref.at[units, :])
        copies.append(
            [
                pltpu.make_async_copy(source, chunk.at[j], sems.at[n, j])
                for n, (source, chunk) in enumerate(zip(sources, chunk_refs))
            ]
        )
    for step in copies:
        for copy in step:
            copy.start()
    return copies


def forward_kernel(experts, waited, router_ref, *refs):
    me = lax.axis_index("ep")
    weight_refs, message_refs = refs[:3], [refs[3].at[me ^ k] for k in range(experts)]
    refs = refs[4 + waited :]
    out_refs = refs[:experts]
    rows_ref, total_ref, gate_ref, up_ref, down_ref, sems, extra_ref, message_sems = refs[experts:]
    arriving = message_copies(message_refs, 0, rows_ref, extra_ref, message_sems)
    copies = weight_copies(weight_refs, (gate_ref, up_ref, down_ref), sems)
    spread(arriving, rows_ref, extra_ref)
    weight = row_weight(rows_ref, router_ref)
    for j, step in enumerate(copies):
        for copy in step:
            copy.wait()
        gate_proj = plain_dot(rows_ref[...], gate_ref[j])
        up_proj = plain_dot(rows_ref[...], up_ref[j])
        hidden = (gate_proj * jax.nn.sigmoid(gate_proj) * up_proj).astype(jnp.bfloat16)
        part = plain_dot(hidden, down_ref[j])
        total_ref[...] = part if j == 0 else total_ref[...] + part
    expert = total_ref[...].astype(jnp.bfloat16).astype(jnp.float32)
    section = rows_ref[...].astype(jnp.float32) + weight * expert
    rows_ref[...] = section.astype(jnp.bfloat16)
    collect(rows_ref, extra_ref, out_refs, message_sems)


def backward_kernel(experts, waited, router_ref, *refs):
    weight_refs = refs[:3]
    message_refs = refs[3 : 3 + experts]
    refs = refs[3 + experts + waited :]
    out_refs = refs[:experts]
    (
        rows_ref,
        total_ref,
        gate_ref,
        up_ref,
        down_ref,
        sems,
        extra_ref,
        message_sems,
        grads_ref,
        weighted_ref,
        grads_extra_ref,
        grad_sems,
    ) = refs[experts:]
    arriving = message_copies(message_refs, 0, rows_ref, extra_ref, message_sems)
    arriving_grads = message_copies(message_refs, 1, grads_ref, grads_extra_ref, grad_sems)
    copies = weight_copies(weight_refs, (gate_ref, up_ref, down_ref), sems)
    spread(arriving, rows_ref, extra_ref)
    spread(arriving_grads, grads_ref, grads_extra_ref)
    weighted = row_weight(rows_ref, router_ref) * grads_ref[...].astype(jnp.float32)
    weighted_ref[...] = weighted.astype(jnp.bfloat16)
    for j, step in enumerate(copies):
        for copy in step:
            copy.wait()
        gate_proj = plain_dot(rows_ref[...], gate_ref[j])
        up_proj = plain_dot(rows_ref[...], up_ref[j])
        d_hidden = transposed_dot(weighted_ref[...], down_ref[j])
        sigmoid_gate = jax.nn.sigmoid(gate_proj)
        d_gate = d_hidden * up_proj * sigmoid_gate * (1.0 + gate_proj * (1.0 - sigmoid_gate))
        d_up = d_hidden * gate_proj * sigmoid_gate
        part = transposed_dot(d_gate.astype(jnp.bfloat16), gate_ref[j])
        part = part + transposed_dot(d_up.astype(jnp.bfloat16), up_ref[j])
        total_ref[...] = part if j == 0 else total_ref[...] + part
    expert = total_ref[...].astype(jnp.bfloat16).astype(jnp.float32)
    section = grads_ref[...].astype(jnp.float32) + expert
    rows_ref[...] = section.astype(jnp.bfloat16)
    collect(rows_ref, extra_ref, out_refs, message_sems)


def pack(ids_rows, sources, kind, experts, joined, after=()):
    tokens, width = sources[0].shape
    dtype = sources[0].dtype
    count = len(sources)
    message = (count * BASE_ROWS, width + width // CUTS)
    slots = count * experts * BASE_ROWS
    anywhere = pl.BlockSpec(memory_space=pl.ANY)
    shapes = [(experts, *message)] if joined else [message] * experts
    return pl.pallas_call(
        functools.partial(pack_kernel, kind, joined, count, experts),
        in_specs=[pl.BlockSpec(memory_space=pltpu.VMEM)] + [anywhere] * (count + len(after)),
        out_specs=[anywhere] * len(shapes),
        out_shape=[jax.ShapeDtypeStruct(shape, dtype) for shape in shapes],
        scratch_shapes=[
            pltpu.VMEM((count, tokens, width), dtype),
            pltpu.VMEM((experts, *message), dtype),
            pltpu.SemaphoreType.DMA((count,)),
            pltpu.SemaphoreType.DMA((experts,)),
        ],
        compiler_params=pltpu.CompilerParams(vmem_limit_bytes=16 << 20),
        cost_estimate=pl.CostEstimate(
            flops=4 * slots * tokens * width,
            bytes_accessed=2 * ROWS_BYTES * slots * width,
            transcendentals=0,
        ),
        name="pack",
    )(ids_rows, *sources, *after)


def unpack(ids_row, messages, order):
    experts = len(order)
    tokens = ids_row.shape[1]
    width = messages[0].shape[1] * CUTS // (CUTS + 1)
    slots = experts * BASE_ROWS
    return pl.pallas_call(
        functools.partial(unpack_kernel, order),
        out_shape=jax.ShapeDtypeStruct((tokens, width), messages[0].dtype),
        compiler_params=pltpu.CompilerParams(vmem_limit_bytes=16 << 20),
        cost_estimate=pl.CostEstimate(
            flops=4 * slots * tokens * width,
            bytes_accessed=2 * ROWS_BYTES * slots * width,
            transcendentals=0,
        ),
        name="unpack",
    )(ids_row, *[messages[k] for k in order])


def expert_call(
    kernel, name, router_rows, gate_cols, up_cols, down_rows, messages, experts, products, after
):
    width, units = gate_cols.shape
    row_count = experts * (BASE_ROWS + CUTS)
    steps = 4 if units % 512 == 0 else 1
    part = units // steps
    result_shape = (BASE_ROWS, messages[0].shape[-1])
    in_vmem = pl.BlockSpec(memory_space=pltpu.VMEM)
    anywhere = pl.BlockSpec(memory_space=pl.ANY)
    rows_scratch = pltpu.VMEM((row_count, width), jnp.bfloat16)
    message_scratch = [
        pltpu.VMEM((experts * BASE_ROWS, width // CUTS), jnp.bfloat16),
        pltpu.SemaphoreType.DMA((2, experts)),
    ]
    return pl.pallas_call(
        functools.partial(kernel, experts, len(after)),
        in_specs=[in_vmem] + [anywhere] * (3 + len(messages) + len(after)),
        out_specs=[anywhere] * experts,
        out_shape=[jax.ShapeDtypeStruct(result_shape, messages[0].dtype)] * experts,
        scratch_shapes=[
            rows_scratch,
            pltpu.VMEM((row_count, width), jnp.float32),
            pltpu.VMEM((steps, width, part), jnp.bfloat16),
            pltpu.VMEM((steps, width, part), jnp.bfloat16),
            pltpu.VMEM((steps, part, width), jnp.bfloat16),
            pltpu.SemaphoreType.DMA((3, steps)),
            *message_scratch,
        ]
        + ([rows_scratch] * 2 + message_scratch if products > 3 else []),
        compiler_params=pltpu.CompilerParams(vmem_limit_bytes=VMEM_BYTES),
        cost_estimate=pl.CostEstimate(
            flops=2 * products * row_count * width * units,
            bytes_accessed=3 * ROWS_BYTES * width * units,
            transcendentals=row_count * units,
        ),
        name=name,
    )(router_rows, gate_cols, up_cols, down_rows, *messages, *after)


def exchanged(messages, order):
    experts = len(messages)
    arrived = list(messages)
    for k in order:
        arrived[k] = lax.ppermute(messages[k], "ep", [(i, i ^ k) for i in range(experts)])
    return arrived


def returned(messages, order, steps):
    sections, experts = lax.axis_size("pp"), len(messages)
    back = list(messages)
    for k in order:
        pairs = [
            (p * experts + e, (p + steps) % sections * experts + (e ^ k))
            for p in range(sections)
            for e in range(experts)
        ]
        back[k] = lax.ppermute(messages[k], ("pp", "ep"), pairs)
    return back


def per_device_whole(fwd_in, fwd_ids, saved_in, bwd_ids, grad_in, router, w_gate, w_up, w_down):
    experts = router.shape[-1]
    token_count = fwd_in.shape[1]
    router_rows = router[0].T
    weights = (w_gate[0], w_up[0], w_down[0])
    ids = jnp.concatenate([array.reshape(1, token_count) for array in (fwd_ids, bwd_ids)], axis=0)
    near, far = list(range(1, experts // 2)), list(range(experts // 2, experts))
    fwd_packed = pack(ids, [fwd_in[0]], 0, experts, True)
    fwd_rows = lax.all_to_all(fwd_packed[0], "ep", split_axis=0, concat_axis=0, tiled=True)
    all_ids = lax.all_gather(ids, "pp")
    section, sections = lax.axis_index("pp"), lax.axis_size("pp")
    fwd_row_next = lax.dynamic_index_in_dim(all_ids, (section + sections - 1) % sections, 0, False)[:1]
    bwd_row_next = lax.dynamic_index_in_dim(all_ids, (section + 1) % sections, 0, False)[1:]
    after = [fwd_packed[0], fwd_row_next, bwd_row_next]
    bwd_packed = pack(ids, [saved_in[0], grad_in[0]], 1, experts, False, after)
    bwd_rows = exchanged(bwd_packed, range(1, experts))
    after = [bwd_rows[k] for k in near]
    fwd_out = expert_call(
        forward_kernel, "forward", router_rows, *weights, [fwd_rows], experts, 3, after
    )
    fwd_back = returned(fwd_out, range(experts), 1)
    after = [fwd_back[k] for k in near + [0]]
    bwd_out = expert_call(
        backward_kernel, "backward", router_rows, *weights, bwd_rows, experts, 5, after
    )
    bwd_back = returned(bwd_out, range(experts), -1)
    fwd_next = unpack(fwd_row_next, fwd_back, near + [0] + far)
    grad_next = unpack(bwd_row_next, bwd_back, near[:1] + far + near[1:] + [0])
    return (fwd_next[None], grad_next[None])


def solution(mesh):
    in_specs = (
        P("pp", "ep", None),
        P("pp", "ep", None),
        P("pp", "ep", None),
        P("pp", "ep", None),
        P("pp", "ep", None),
        P("pp", None, None),
        P("pp", None, "ep"),
        P("pp", None, "ep"),
        P("pp", "ep", None),
    )
    out_specs = (P("pp", "ep", None), P("pp", "ep", None))

    def layer(*arrays):
        token_count = arrays[0].shape[1] // mesh.shape["ep"]
        width = arrays[0].shape[2]
        experts = arrays[5].shape[-1]
        whole = (
            mesh.shape["ep"] == experts
            and experts & (experts - 1) == 0
            and 5 * token_count // (4 * experts) == BASE_ROWS + CUTS
            and width % (128 * CUTS) == 0
        )
        return jax.shard_map(
            per_device_whole if whole else per_device,
            mesh=mesh,
            in_specs=in_specs,
            out_specs=out_specs,
            check_vma=False,
        )(*arrays)

    return layer
```

```python
import functools

import jax
import jax.numpy as jnp
from jax import lax
from jax.experimental import pallas as pl
from jax.experimental.pallas import tpu as pltpu
from jax.sharding import PartitionSpec as P

route_scale = 2.5
contract = (((1,), (1,)), ((), ()))


def shortened(value):

    def short(part):
        return part.astype(jnp.bfloat16) if part.dtype == jnp.float32 else part

    return jax.tree.map(short, value)


def swapped(value, axis, distance):
    return lax.ppermute(value, axis, [(i, i ^ 1 << distance) for i in range(lax.axis_size(axis))])


def from_behind(value, axis, steps):
    count = lax.axis_size(axis)
    pairs = [(source, (source + steps) % count) for source in range(count)]
    return lax.ppermute(value, axis, pairs)


def order_slots(chosen, experts, capacity):
    token_count = chosen.shape[0]
    onehot = (chosen[:, None] == jnp.arange(experts, dtype=jnp.int32)[None, :]).astype(jnp.int32)
    before = jnp.cumsum(onehot, axis=0) - onehot
    ranking = jnp.sum(before * onehot, axis=1)
    slot_table = jnp.full((experts * capacity,), token_count, jnp.int32)
    slot_table = slot_table.at[chosen * capacity + ranking].set(
        jnp.arange(token_count, dtype=jnp.int32)
    )
    return (onehot, ranking, slot_table)


def routing_weight(tokens, router, onehot):
    logits = jnp.dot(tokens.astype(jnp.float32), router, precision=lax.Precision.HIGHEST)
    picked = jnp.sum(jnp.where(onehot > 0, logits, 0.0), axis=1)
    return route_scale * jax.nn.sigmoid(picked)


def with_zero_row(tokens):
    return jnp.concatenate([tokens, jnp.zeros((1, tokens.shape[1]), tokens.dtype)], axis=0)


def expert_forward(row_block, gate_cols, up_cols, down_rows):
    gate_proj = jnp.dot(row_block, gate_cols, preferred_element_type=jnp.float32)
    up_proj = jnp.dot(row_block, up_cols, preferred_element_type=jnp.float32)
    hidden = (gate_proj * jax.nn.sigmoid(gate_proj) * up_proj).astype(jnp.bfloat16)
    return jnp.dot(hidden, down_rows, preferred_element_type=jnp.float32).astype(jnp.bfloat16)


def expert_backward(row_block, row_grads, joined_cols, down_rows):
    unit_count = down_rows.shape[0]
    both_proj = jnp.dot(row_block, joined_cols, preferred_element_type=jnp.float32)
    gate_proj = both_proj[:, :unit_count]
    up_proj = both_proj[:, unit_count:]
    d_hidden = lax.dot_general(row_grads, down_rows, contract, preferred_element_type=jnp.float32)
    sigmoid_gate = jax.nn.sigmoid(gate_proj)
    d_gate = (d_hidden * up_proj * sigmoid_gate * (1.0 + gate_proj * (1.0 - sigmoid_gate))).astype(
        jnp.bfloat16
    )
    d_up = (d_hidden * gate_proj * sigmoid_gate).astype(jnp.bfloat16)
    d_joined = jnp.concatenate([d_gate, d_up], axis=1)
    partial_sum = lax.dot_general(
        d_joined, joined_cols, contract, preferred_element_type=jnp.float32
    )
    return partial_sum.astype(jnp.bfloat16)


def arrange(own_rows, peer_rows, own_bit):
    return jnp.where(
        own_bit == 0, jnp.stack([own_rows, peer_rows]), jnp.stack([peer_rows, own_rows])
    )


def per_device(fwd_in, fwd_ids, saved_in, bwd_ids, grad_in, router, w_gate, w_up, w_down):
    experts = router.shape[-1]
    owners = lax.axis_size("ep")
    group_size = owners // experts
    bit_count = group_size.bit_length() - 1
    own_index = lax.axis_index("ep")
    token_count = fwd_in.shape[1]
    width = fwd_in.shape[2]
    capacity = group_size * max(1, 5 * token_count // (4 * experts * group_size))
    quarter_slots = capacity // group_size
    router_section = router[0]
    gate_cols = w_gate[0]
    up_cols = w_up[0]
    down_rows = w_down[0]
    joined_cols = jnp.concatenate([gate_cols, up_cols], axis=1)
    fwd_tokens = fwd_in[0]
    fwd_chosen = fwd_ids[0, :, 0]
    fwd_onehot, fwd_rank, fwd_table = order_slots(fwd_chosen, experts, capacity)
    fwd_weight = routing_weight(fwd_tokens, router_section, fwd_onehot)
    fwd_padded = with_zero_row(fwd_tokens)
    saved_tokens = saved_in[0]
    bwd_chosen = bwd_ids[0, :, 0]
    grad_tokens = grad_in[0]
    bwd_onehot, bwd_rank, bwd_table = order_slots(bwd_chosen, experts, capacity)
    bwd_weight = routing_weight(saved_tokens, router_section, bwd_onehot)
    weighted = (bwd_weight[:, None] * grad_tokens.astype(jnp.float32)).astype(jnp.bfloat16)
    saved_padded = with_zero_row(saved_tokens)
    weighted_padded = with_zero_row(weighted)
    fwd_index = (
        fwd_table.reshape(experts, quarter_slots, group_size)
        .transpose(0, 2, 1)
        .reshape(owners, quarter_slots)
    )
    gathered = lax.all_to_all(
        jnp.take(fwd_padded, fwd_index, axis=0), "ep", split_axis=0, concat_axis=0, tiled=True
    )
    for bit_number in range(bit_count):
        own_bit = own_index >> bit_number & 1
        peer_rows = swapped(shortened(gathered), "ep", bit_number).astype(gathered.dtype)
        gathered = arrange(gathered, peer_rows, own_bit)
    partial_out = expert_forward(gathered.reshape(-1, width), gate_cols, up_cols, down_rows)
    partial_out = partial_out.reshape(group_size, 1, owners * quarter_slots, width)
    for bit_number in reversed(range(bit_count)):
        own_bit = own_index >> bit_number & 1
        half_rows = partial_out.shape[0] // 2
        kept_half = lax.dynamic_slice_in_dim(partial_out, own_bit * half_rows, half_rows, 0)
        sent_half = lax.dynamic_slice_in_dim(partial_out, (1 - own_bit) * half_rows, half_rows, 0)
        partial_out = jnp.concatenate([kept_half, swapped(sent_half, "ep", bit_number)], axis=1)
    summed = jnp.sum(partial_out, axis=(0, 1), dtype=jnp.float32).astype(jnp.bfloat16)
    returned = lax.all_to_all(
        summed.reshape(owners, quarter_slots, width), "ep", split_axis=0, concat_axis=0, tiled=True
    ).reshape(-1, width)
    source_slot = (
        fwd_chosen * group_size + fwd_rank % group_size
    ) * quarter_slots + fwd_rank // group_size
    fwd_expert = jnp.take(returned, source_slot, axis=0).astype(jnp.float32)
    bwd_index = (
        bwd_table.reshape(experts, quarter_slots, group_size)
        .transpose(0, 2, 1)
        .reshape(owners, quarter_slots)
    )
    saved_rows, grad_rows = (
        lax.all_to_all(
            jnp.take(saved_padded, bwd_index, axis=0), "ep", split_axis=0, concat_axis=0, tiled=True
        ),
        lax.all_to_all(
            jnp.take(weighted_padded, bwd_index, axis=0),
            "ep",
            split_axis=0,
            concat_axis=0,
            tiled=True,
        ),
    )
    for bit_number in range(bit_count):
        own_bit = own_index >> bit_number & 1
        peer_saved, peer_grads = (
            swapped(shortened(saved_rows), "ep", bit_number).astype(saved_rows.dtype),
            swapped(shortened(grad_rows), "ep", bit_number).astype(grad_rows.dtype),
        )
        saved_rows = arrange(saved_rows, peer_saved, own_bit)
        grad_rows = arrange(grad_rows, peer_grads, own_bit)
    partial_grad = expert_backward(
        saved_rows.reshape(-1, width), grad_rows.reshape(-1, width), joined_cols, down_rows
    )
    partial_grad = partial_grad.reshape(group_size, 1, owners * quarter_slots, width)
    for bit_number in reversed(range(bit_count)):
        own_bit = own_index >> bit_number & 1
        half_rows = partial_grad.shape[0] // 2
        kept_half = lax.dynamic_slice_in_dim(partial_grad, own_bit * half_rows, half_rows, 0)
        sent_half = lax.dynamic_slice_in_dim(partial_grad, (1 - own_bit) * half_rows, half_rows, 0)
        partial_grad = jnp.concatenate([kept_half, swapped(sent_half, "ep", bit_number)], axis=1)
    summed_grad = jnp.sum(partial_grad, axis=(0, 1), dtype=jnp.float32).astype(jnp.bfloat16)
    returned_grad = lax.all_to_all(
        summed_grad.reshape(owners, quarter_slots, width),
        "ep",
        split_axis=0,
        concat_axis=0,
        tiled=True,
    ).reshape(-1, width)
    grad_slot = (
        bwd_chosen * group_size + bwd_rank % group_size
    ) * quarter_slots + bwd_rank // group_size
    bwd_expert = jnp.take(returned_grad, grad_slot, axis=0).astype(jnp.float32)
    fwd_section = (fwd_tokens.astype(jnp.float32) + fwd_weight[:, None] * fwd_expert).astype(
        jnp.bfloat16
    )
    grad_section = (grad_tokens.astype(jnp.float32) + bwd_expert).astype(jnp.bfloat16)
    fwd_next = from_behind(fwd_section[None], "pp", 1)
    grad_next = from_behind(grad_section[None], "pp", -1)
    return (fwd_next, grad_next)


BASE_ROWS = 16
CUTS = 4
COLUMNS = 512
ROWS_BYTES = 2
VMEM_BYTES = 44 << 20
PACK_BYTES = 60 << 20


def transposed_dot(left, right):
    return lax.dot_general(left, right, contract, preferred_element_type=jnp.float32)


def plain_dot(left, right):
    return jnp.dot(left, right, preferred_element_type=jnp.float32)


def slot_masks(ids_row, me, experts):
    tokens = ids_row.shape[1]
    wanted = lax.broadcasted_iota(jnp.int32, (experts, tokens), 0) == ids_row
    chosen = jnp.where(wanted, 1.0, 0.0)
    earlier = jnp.where(
        lax.broadcasted_iota(jnp.int32, (tokens, tokens), 0)
        < lax.broadcasted_iota(jnp.int32, (tokens, tokens), 1),
        1.0,
        0.0,
    )
    before = plain_dot(chosen.astype(jnp.bfloat16), earlier.astype(jnp.bfloat16))
    rank = jnp.sum(before * chosen, axis=0, keepdims=True).astype(jnp.int32)
    row = lax.broadcasted_iota(jnp.int32, (experts * BASE_ROWS, tokens), 0)
    mine = ids_row == ((row // BASE_ROWS) ^ me)
    place = row % BASE_ROWS
    base = jnp.where(mine & (rank == place), 1.0, 0.0).astype(jnp.bfloat16)
    extra = mine & (rank == BASE_ROWS + place % CUTS)
    pieces = [
        jnp.where(extra & (place // CUTS == q), 1.0, 0.0).astype(jnp.bfloat16) for q in range(CUTS)
    ]
    return base, pieces


def pack_kernel(joined, count, experts, own_ids_ref, *refs):
    x_refs = refs[:count]
    held_ref, made_ref, sems, out_sems, ids_ref, ids_sem = refs[-6:]
    refs = refs[:-2]
    ids_copy = pltpu.make_async_copy(own_ids_ref, ids_ref, ids_sem)
    ids_copy.start()
    copies = [pltpu.make_async_copy(x_refs[n], held_ref.at[n], sems.at[n]) for n in range(count)]
    for copy in copies:
        copy.start()
    width = held_ref.shape[2]
    piece = width // CUTS
    first = 0 if joined else lax.axis_index("ep")
    ids_copy.wait()
    base, pieces = slot_masks(ids_ref[...], first, experts)
    for n, copy in enumerate(copies):
        rows = slice(n * BASE_ROWS, (n + 1) * BASE_ROWS)
        copy.wait()
        extra = 0.0
        for q in range(CUTS):
            columns = slice(q * piece, (q + 1) * piece)
            part = held_ref[n, :, columns]
            packed = plain_dot(base, part).astype(jnp.bfloat16)
            extra = extra + plain_dot(pieces[q], part)
            for k in range(experts):
                made_ref[k, rows, columns] = packed[k * BASE_ROWS : (k + 1) * BASE_ROWS]
        extra = extra.astype(jnp.bfloat16)
        for k in range(experts):
            made_ref[k, rows, width:] = extra[k * BASE_ROWS : (k + 1) * BASE_ROWS]
    if joined:
        copies = [pltpu.make_async_copy(made_ref, refs[-5], out_sems.at[0])]
    else:
        out_refs = refs[-4 - experts : -4]
        copies = [
            pltpu.make_async_copy(made_ref.at[k], out_refs[k], out_sems.at[k]) for k in range(experts)
        ]
    for copy in copies:
        copy.start()
    for copy in copies:
        copy.wait()


def unpack_kernel(order, ids_ref, *refs):
    me = lax.axis_index("ep")
    experts = len(order)
    message_refs, out_ref = [refs[order.index(k)] for k in range(experts)], refs[experts]
    width = out_ref.shape[1]
    piece = width // CUTS
    base, pieces = slot_masks(ids_ref[...], me, experts)
    from_rows = (((0,), (0,)), ((), ()))
    extra = jnp.concatenate([ref[:, width:] for ref in message_refs], axis=0)
    for q in range(CUTS):
        columns = slice(q * piece, (q + 1) * piece)
        rows = jnp.concatenate([ref[:, columns] for ref in message_refs], axis=0)
        total = lax.dot_general(base, rows, from_rows, preferred_element_type=jnp.float32)
        total = total + lax.dot_general(
            pieces[q], extra, from_rows, preferred_element_type=jnp.float32
        )
        out_ref[:, columns] = total.astype(jnp.bfloat16)


def piece_places(experts, q):
    shape = (experts * CUTS, experts * BASE_ROWS)
    slot = lax.broadcasted_iota(jnp.int32, shape, 0)
    row = lax.broadcasted_iota(jnp.int32, shape, 1)
    same = (slot // CUTS == row // BASE_ROWS) & (row % BASE_ROWS == q * CUTS + slot % CUTS)
    return jnp.where(same, 1.0, 0.0).astype(jnp.bfloat16)


def message_copies(message_refs, place, rows_ref, extra_ref, sems):
    width = rows_ref.shape[1]
    taken = slice(place * BASE_ROWS, (place + 1) * BASE_ROWS)
    copies = []
    for k, ref in enumerate(message_refs):
        rows = slice(k * BASE_ROWS, (k + 1) * BASE_ROWS)
        parts = ((ref.at[taken, :width], rows_ref), (ref.at[taken, width:], extra_ref))
        for n, (source, target) in enumerate(parts):
            copies.append(pltpu.make_async_copy(source, target.at[rows, :], sems.at[n, k]))
    for copy in copies:
        copy.start()
    return copies


def spread(copies, rows_ref, extra_ref):
    width = rows_ref.shape[1]
    piece = width // CUTS
    experts = extra_ref.shape[0] // BASE_ROWS
    for copy in copies:
        copy.wait()
    for q in range(CUTS):
        picked = plain_dot(piece_places(experts, q), extra_ref[...])
        columns = slice(q * piece, (q + 1) * piece)
        rows_ref[experts * BASE_ROWS :, columns] = picked.astype(jnp.bfloat16)


def collect(rows_ref, extra_ref, message_refs, sems):
    experts = len(message_refs)
    width = rows_ref.shape[1]
    piece = width // CUTS
    first = experts * BASE_ROWS
    from_rows = (((0,), (0,)), ((), ()))
    extra = 0.0
    for q in range(CUTS):
        extra = extra + lax.dot_general(
            piece_places(experts, q),
            rows_ref[first:, q * piece : (q + 1) * piece],
            from_rows,
            preferred_element_type=jnp.float32,
        )
    extra_ref[...] = extra.astype(jnp.bfloat16)
    copies = []
    for k, ref in enumerate(message_refs):
        rows = slice(k * BASE_ROWS, (k + 1) * BASE_ROWS)
        parts = ((rows_ref, ref.at[:, :width]), (extra_ref, ref.at[:, width:]))
        for n, (source, target) in enumerate(parts):
            copies.append(pltpu.make_async_copy(source.at[rows, :], target, sems.at[n, k]))
    for copy in copies:
        copy.start()
    for copy in copies:
        copy.wait()


def column_loop(width, step, body):
    for n in range(width // step):
        body(pl.ds(n * step, step))


def row_weight(rows_ref, router_ref):
    row_count, width = rows_ref.shape
    experts = router_ref.shape[0]
    own = lax.broadcasted_iota(jnp.int32, (experts, 128), 0) == lax.axis_index("ep")

    def add(n, total):
        lanes = pl.ds(pl.multiple_of(n * 128, 128), 128)
        centroid = jnp.sum(jnp.where(own, router_ref[:, lanes], 0.0), axis=0, keepdims=True)
        return total + rows_ref[:, lanes].astype(jnp.float32) * centroid

    total = lax.fori_loop(0, width // 128, add, jnp.zeros((row_count, 128), jnp.float32), unroll=4)
    return route_scale * jax.nn.sigmoid(jnp.sum(total, axis=1, keepdims=True))


def weight_copies(weight_refs, held_refs, sems):
    gate_ref, up_ref, down_ref = weight_refs
    steps = sems.shape[1]
    part = gate_ref.shape[1] // steps

    def copies(j):
        units = pl.ds(pl.multiple_of(j * part, part), part)
        places = ((slice(None), units), (slice(None), units), (units, slice(None)))
        return [
            pltpu.make_async_copy(source.at[place], held.at[place], sems.at[n, j])
            for n, (source, held, place) in enumerate(zip(weight_refs, held_refs, places))
        ]

    for j in range(steps):
        for copy in copies(j):
            copy.start()

    def wait(j):
        for copy in copies(j):
            copy.wait()

    return wait


def unit_loop(sems, units, body):
    steps = sems.shape[1]
    part = units // steps

    for j in range(steps):
        body(j, pl.ds(j * part, part))


def forward_kernel(experts, waited, router_ref, *refs):
    me = lax.axis_index("ep")
    weight_refs, message_refs = refs[:3], [refs[3].at[me ^ k] for k in range(experts)]
    refs = refs[4 + waited :]
    out_refs = refs[:experts]
    rows_ref, gate_ref, up_ref, down_ref, sems, extra_ref, message_sems, total_ref = refs[experts:]
    arriving = message_copies(message_refs, 0, rows_ref, extra_ref, message_sems)
    wait = weight_copies(weight_refs, (gate_ref, up_ref, down_ref), sems)
    spread(arriving, rows_ref, extra_ref)
    weight = row_weight(rows_ref, router_ref)

    def project(j, units):
        wait(j)
        gate_proj = plain_dot(rows_ref[...], gate_ref[:, units])
        up_proj = plain_dot(rows_ref[...], up_ref[:, units])
        hidden = (gate_proj * jax.nn.sigmoid(gate_proj) * up_proj).astype(jnp.bfloat16)
        part = plain_dot(hidden, down_ref[units, :])
        total_ref[...] = part if j == 0 else total_ref[...] + part

    unit_loop(sems, gate_ref.shape[1], project)
    expert = total_ref[...].astype(jnp.bfloat16).astype(jnp.float32)
    section = rows_ref[...].astype(jnp.float32) + weight * expert
    rows_ref[...] = section.astype(jnp.bfloat16)
    collect(rows_ref, extra_ref, out_refs, message_sems)


def backward_kernel(experts, waited, router_ref, *refs):
    weight_refs = refs[:3]
    message_refs = refs[3 : 3 + experts]
    refs = refs[3 + experts + waited :]
    out_refs = refs[:experts]
    (
        rows_ref,
        gate_ref,
        up_ref,
        down_ref,
        sems,
        extra_ref,
        message_sems,
        d_gate_ref,
        d_up_ref,
        grads_ref,
        weighted_ref,
        grads_extra_ref,
        grad_sems,
    ) = refs[experts:]
    arriving = message_copies(message_refs, 0, rows_ref, extra_ref, message_sems)
    arriving_grads = message_copies(message_refs, 1, grads_ref, grads_extra_ref, grad_sems)
    wait = weight_copies(weight_refs, (gate_ref, up_ref, down_ref), sems)
    spread(arriving, rows_ref, extra_ref)
    spread(arriving_grads, grads_ref, grads_extra_ref)
    weight = row_weight(rows_ref, router_ref)

    def weigh(columns):
        weighted = weight * grads_ref[:, columns].astype(jnp.float32)
        weighted_ref[:, columns] = weighted.astype(jnp.bfloat16)

    def project(j, units):
        wait(j)
        gate_proj = plain_dot(rows_ref[...], gate_ref[:, units])
        up_proj = plain_dot(rows_ref[...], up_ref[:, units])
        d_hidden = transposed_dot(weighted_ref[...], down_ref[units, :])
        sigmoid_gate = jax.nn.sigmoid(gate_proj)
        d_gate = d_hidden * up_proj * sigmoid_gate * (1.0 + gate_proj * (1.0 - sigmoid_gate))
        d_up = d_hidden * gate_proj * sigmoid_gate
        d_gate_ref[:, units] = d_gate.astype(jnp.bfloat16)
        d_up_ref[:, units] = d_up.astype(jnp.bfloat16)

    def finish(columns):
        total = transposed_dot(d_gate_ref[...], gate_ref[columns, :])
        total = total + transposed_dot(d_up_ref[...], up_ref[columns, :])
        expert = total.astype(jnp.bfloat16).astype(jnp.float32)
        section = grads_ref[:, columns].astype(jnp.float32) + expert
        rows_ref[:, columns] = section.astype(jnp.bfloat16)

    column_loop(rows_ref.shape[1], COLUMNS, weigh)
    unit_loop(sems, d_gate_ref.shape[1], project)
    column_loop(rows_ref.shape[1], COLUMNS, finish)
    collect(rows_ref, extra_ref, out_refs, message_sems)


def pack(ids_row, sources, experts, joined, after=()):
    tokens, width = sources[0].shape
    dtype = sources[0].dtype
    count = len(sources)
    message = (count * BASE_ROWS, width + width // CUTS)
    slots = count * experts * BASE_ROWS
    anywhere = pl.BlockSpec(memory_space=pl.ANY)
    shapes = [(experts, *message)] if joined else [message] * experts
    return pl.pallas_call(
        functools.partial(pack_kernel, joined, count, experts),
        in_specs=[anywhere] * (1 + count + len(after)),
        out_specs=[anywhere] * len(shapes),
        out_shape=[jax.ShapeDtypeStruct(shape, dtype) for shape in shapes],
        scratch_shapes=[
            pltpu.VMEM((count, tokens, width), dtype),
            pltpu.VMEM((experts, *message), dtype),
            pltpu.SemaphoreType.DMA((count,)),
            pltpu.SemaphoreType.DMA((experts,)),
            pltpu.VMEM(ids_row.shape, ids_row.dtype),
            pltpu.SemaphoreType.DMA(()),
        ],
        compiler_params=pltpu.CompilerParams(vmem_limit_bytes=PACK_BYTES),
        cost_estimate=pl.CostEstimate(
            flops=4 * slots * tokens * width,
            bytes_accessed=2 * ROWS_BYTES * slots * width,
            transcendentals=0,
        ),
        name="pack",
    )(ids_row, *sources, *after)


def unpack(ids_row, messages, order):
    experts = len(order)
    tokens = ids_row.shape[1]
    width = messages[0].shape[1] * CUTS // (CUTS + 1)
    slots = experts * BASE_ROWS
    return pl.pallas_call(
        functools.partial(unpack_kernel, order),
        out_shape=jax.ShapeDtypeStruct((tokens, width), messages[0].dtype),
        compiler_params=pltpu.CompilerParams(vmem_limit_bytes=16 << 20),
        cost_estimate=pl.CostEstimate(
            flops=4 * slots * tokens * width,
            bytes_accessed=2 * ROWS_BYTES * slots * width,
            transcendentals=0,
        ),
        name="unpack",
    )(ids_row, *[messages[k] for k in order])


def expert_call(
    kernel, name, router_rows, gate_cols, up_cols, down_rows, messages, experts, products, after
):
    width, units = gate_cols.shape
    row_count = experts * (BASE_ROWS + CUTS)
    steps = 4 if units % 512 == 0 else 1
    result_shape = (BASE_ROWS, messages[0].shape[-1])
    in_vmem = pl.BlockSpec(memory_space=pltpu.VMEM)
    anywhere = pl.BlockSpec(memory_space=pl.ANY)
    rows_scratch = pltpu.VMEM((row_count, width), jnp.bfloat16)
    message_scratch = [
        pltpu.VMEM((experts * BASE_ROWS, width // CUTS), jnp.bfloat16),
        pltpu.SemaphoreType.DMA((2, experts)),
    ]
    if products > 3:
        own_scratch = [pltpu.VMEM((row_count, units), jnp.bfloat16)] * 2
        own_scratch += [rows_scratch] * 2 + message_scratch
    else:
        own_scratch = [pltpu.VMEM((row_count, width), jnp.float32)]
    return pl.pallas_call(
        functools.partial(kernel, experts, len(after)),
        in_specs=[in_vmem] + [anywhere] * (3 + len(messages) + len(after)),
        out_specs=[anywhere] * experts,
        out_shape=[jax.ShapeDtypeStruct(result_shape, messages[0].dtype)] * experts,
        scratch_shapes=[
            rows_scratch,
            pltpu.VMEM((width, units), jnp.bfloat16),
            pltpu.VMEM((width, units), jnp.bfloat16),
            pltpu.VMEM((units, width), jnp.bfloat16),
            pltpu.SemaphoreType.DMA((3, steps)),
            *message_scratch,
            *own_scratch,
        ],
        compiler_params=pltpu.CompilerParams(vmem_limit_bytes=VMEM_BYTES),
        cost_estimate=pl.CostEstimate(
            flops=2 * products * row_count * width * units,
            bytes_accessed=3 * ROWS_BYTES * width * units,
            transcendentals=row_count * units,
        ),
        name=name,
    )(router_rows, gate_cols, up_cols, down_rows, *messages, *after)


def exchanged(messages, order):
    experts = len(messages)
    arrived = list(messages)
    for k in order:
        arrived[k] = lax.ppermute(messages[k], "ep", [(i, i ^ k) for i in range(experts)])
    return arrived


def returned(messages, order, steps):
    sections, experts = lax.axis_size("pp"), len(messages)
    back = list(messages)
    for k in order:
        pairs = [
            (p * experts + e, (p + steps) % sections * experts + (e ^ k))
            for p in range(sections)
            for e in range(experts)
        ]
        back[k] = lax.ppermute(messages[k], ("pp", "ep"), pairs)
    return back


def per_device_whole(fwd_in, fwd_ids, saved_in, bwd_ids, grad_in, router, w_gate, w_up, w_down):
    experts = router.shape[-1]
    token_count = fwd_in.shape[1]
    router_rows = router[0].T
    weights = (w_gate[0], w_up[0], w_down[0])
    fwd_row, bwd_row = fwd_ids.reshape(1, token_count), bwd_ids.reshape(1, token_count)
    near, far = list(range(1, experts // 2)), list(range(experts // 2, experts))
    fwd_packed = pack(fwd_row, [fwd_in[0]], experts, True)
    fwd_rows = lax.all_to_all(fwd_packed[0], "ep", split_axis=0, concat_axis=0, tiled=True)
    all_ids = lax.all_gather(jnp.concatenate([fwd_row, bwd_row], axis=0), "pp")
    section, sections = lax.axis_index("pp"), lax.axis_size("pp")
    fwd_row_next = lax.dynamic_index_in_dim(all_ids, (section + sections - 1) % sections, 0, False)[:1]
    bwd_row_next = lax.dynamic_index_in_dim(all_ids, (section + 1) % sections, 0, False)[1:]
    after = [fwd_packed[0], fwd_row_next, bwd_row_next]
    bwd_packed = pack(bwd_row, [saved_in[0], grad_in[0]], experts, False, after)
    bwd_rows = exchanged(bwd_packed, range(1, experts))
    after = [bwd_rows[k] for k in near]
    fwd_out = expert_call(
        forward_kernel, "forward", router_rows, *weights, [fwd_rows], experts, 3, after
    )
    fwd_back = returned(fwd_out, range(experts), 1)
    after = [fwd_back[k] for k in near + [0]]
    bwd_out = expert_call(
        backward_kernel, "backward", router_rows, *weights, bwd_rows, experts, 5, after
    )
    bwd_back = returned(bwd_out, range(experts), -1)
    fwd_next = unpack(fwd_row_next, fwd_back, near + [0] + far)
    grad_next = unpack(bwd_row_next, bwd_back, far[:1] + near[:1] + far[1:] + near[1:] + [0])
    return (fwd_next[None], grad_next[None])


def solution(mesh):
    in_specs = (
        P("pp", "ep", None),
        P("pp", "ep", None),
        P("pp", "ep", None),
        P("pp", "ep", None),
        P("pp", "ep", None),
        P("pp", None, None),
        P("pp", None, "ep"),
        P("pp", None, "ep"),
        P("pp", "ep", None),
    )
    out_specs = (P("pp", "ep", None), P("pp", "ep", None))

    def layer(*arrays):
        token_count = arrays[0].shape[1] // mesh.shape["ep"]
        width = arrays[0].shape[2]
        experts = arrays[5].shape[-1]
        whole = (
            mesh.shape["ep"] == experts
            and experts & (experts - 1) == 0
            and 5 * token_count // (4 * experts) == BASE_ROWS + CUTS
            and width % (128 * CUTS) == 0
        )
        return jax.shard_map(
            per_device_whole if whole else per_device,
            mesh=mesh,
            in_specs=in_specs,
            out_specs=out_specs,
            check_vma=False,
        )(*arrays)

    return layer
```

```python
import functools

import jax
import jax.numpy as jnp
from jax import lax
from jax.experimental import pallas as pl
from jax.experimental.pallas import tpu as pltpu
from jax.sharding import PartitionSpec as P

route_scale = 2.5
contract = (((1,), (1,)), ((), ()))


def shortened(value):

    def short(part):
        return part.astype(jnp.bfloat16) if part.dtype == jnp.float32 else part

    return jax.tree.map(short, value)


def swapped(value, axis, distance):
    return lax.ppermute(value, axis, [(i, i ^ 1 << distance) for i in range(lax.axis_size(axis))])


def from_behind(value, axis, steps):
    count = lax.axis_size(axis)
    pairs = [(source, (source + steps) % count) for source in range(count)]
    return lax.ppermute(value, axis, pairs)


def order_slots(chosen, experts, capacity):
    token_count = chosen.shape[0]
    onehot = (chosen[:, None] == jnp.arange(experts, dtype=jnp.int32)[None, :]).astype(jnp.int32)
    before = jnp.cumsum(onehot, axis=0) - onehot
    ranking = jnp.sum(before * onehot, axis=1)
    slot_table = jnp.full((experts * capacity,), token_count, jnp.int32)
    slot_table = slot_table.at[chosen * capacity + ranking].set(
        jnp.arange(token_count, dtype=jnp.int32)
    )
    return (onehot, ranking, slot_table)


def routing_weight(tokens, router, onehot):
    logits = jnp.dot(tokens.astype(jnp.float32), router, precision=lax.Precision.HIGHEST)
    picked = jnp.sum(jnp.where(onehot > 0, logits, 0.0), axis=1)
    return route_scale * jax.nn.sigmoid(picked)


def with_zero_row(tokens):
    return jnp.concatenate([tokens, jnp.zeros((1, tokens.shape[1]), tokens.dtype)], axis=0)


def expert_forward(row_block, gate_cols, up_cols, down_rows):
    gate_proj = jnp.dot(row_block, gate_cols, preferred_element_type=jnp.float32)
    up_proj = jnp.dot(row_block, up_cols, preferred_element_type=jnp.float32)
    hidden = (gate_proj * jax.nn.sigmoid(gate_proj) * up_proj).astype(jnp.bfloat16)
    return jnp.dot(hidden, down_rows, preferred_element_type=jnp.float32).astype(jnp.bfloat16)


def expert_backward(row_block, row_grads, joined_cols, down_rows):
    unit_count = down_rows.shape[0]
    both_proj = jnp.dot(row_block, joined_cols, preferred_element_type=jnp.float32)
    gate_proj = both_proj[:, :unit_count]
    up_proj = both_proj[:, unit_count:]
    d_hidden = lax.dot_general(row_grads, down_rows, contract, preferred_element_type=jnp.float32)
    sigmoid_gate = jax.nn.sigmoid(gate_proj)
    d_gate = (d_hidden * up_proj * sigmoid_gate * (1.0 + gate_proj * (1.0 - sigmoid_gate))).astype(
        jnp.bfloat16
    )
    d_up = (d_hidden * gate_proj * sigmoid_gate).astype(jnp.bfloat16)
    d_joined = jnp.concatenate([d_gate, d_up], axis=1)
    partial_sum = lax.dot_general(
        d_joined, joined_cols, contract, preferred_element_type=jnp.float32
    )
    return partial_sum.astype(jnp.bfloat16)


def arrange(own_rows, peer_rows, own_bit):
    return jnp.where(
        own_bit == 0, jnp.stack([own_rows, peer_rows]), jnp.stack([peer_rows, own_rows])
    )


def per_device(fwd_in, fwd_ids, saved_in, bwd_ids, grad_in, router, w_gate, w_up, w_down):
    experts = router.shape[-1]
    owners = lax.axis_size("ep")
    group_size = owners // experts
    bit_count = group_size.bit_length() - 1
    own_index = lax.axis_index("ep")
    token_count = fwd_in.shape[1]
    width = fwd_in.shape[2]
    capacity = group_size * max(1, 5 * token_count // (4 * experts * group_size))
    quarter_slots = capacity // group_size
    router_section = router[0]
    gate_cols = w_gate[0]
    up_cols = w_up[0]
    down_rows = w_down[0]
    joined_cols = jnp.concatenate([gate_cols, up_cols], axis=1)
    fwd_tokens = fwd_in[0]
    fwd_chosen = fwd_ids[0, :, 0]
    fwd_onehot, fwd_rank, fwd_table = order_slots(fwd_chosen, experts, capacity)
    fwd_weight = routing_weight(fwd_tokens, router_section, fwd_onehot)
    fwd_padded = with_zero_row(fwd_tokens)
    saved_tokens = saved_in[0]
    bwd_chosen = bwd_ids[0, :, 0]
    grad_tokens = grad_in[0]
    bwd_onehot, bwd_rank, bwd_table = order_slots(bwd_chosen, experts, capacity)
    bwd_weight = routing_weight(saved_tokens, router_section, bwd_onehot)
    weighted = (bwd_weight[:, None] * grad_tokens.astype(jnp.float32)).astype(jnp.bfloat16)
    saved_padded = with_zero_row(saved_tokens)
    weighted_padded = with_zero_row(weighted)
    fwd_index = (
        fwd_table.reshape(experts, quarter_slots, group_size)
        .transpose(0, 2, 1)
        .reshape(owners, quarter_slots)
    )
    gathered = lax.all_to_all(
        jnp.take(fwd_padded, fwd_index, axis=0), "ep", split_axis=0, concat_axis=0, tiled=True
    )
    for bit_number in range(bit_count):
        own_bit = own_index >> bit_number & 1
        peer_rows = swapped(shortened(gathered), "ep", bit_number).astype(gathered.dtype)
        gathered = arrange(gathered, peer_rows, own_bit)
    partial_out = expert_forward(gathered.reshape(-1, width), gate_cols, up_cols, down_rows)
    partial_out = partial_out.reshape(group_size, 1, owners * quarter_slots, width)
    for bit_number in reversed(range(bit_count)):
        own_bit = own_index >> bit_number & 1
        half_rows = partial_out.shape[0] // 2
        kept_half = lax.dynamic_slice_in_dim(partial_out, own_bit * half_rows, half_rows, 0)
        sent_half = lax.dynamic_slice_in_dim(partial_out, (1 - own_bit) * half_rows, half_rows, 0)
        partial_out = jnp.concatenate([kept_half, swapped(sent_half, "ep", bit_number)], axis=1)
    summed = jnp.sum(partial_out, axis=(0, 1), dtype=jnp.float32).astype(jnp.bfloat16)
    returned = lax.all_to_all(
        summed.reshape(owners, quarter_slots, width), "ep", split_axis=0, concat_axis=0, tiled=True
    ).reshape(-1, width)
    source_slot = (
        fwd_chosen * group_size + fwd_rank % group_size
    ) * quarter_slots + fwd_rank // group_size
    fwd_expert = jnp.take(returned, source_slot, axis=0).astype(jnp.float32)
    bwd_index = (
        bwd_table.reshape(experts, quarter_slots, group_size)
        .transpose(0, 2, 1)
        .reshape(owners, quarter_slots)
    )
    saved_rows, grad_rows = (
        lax.all_to_all(
            jnp.take(saved_padded, bwd_index, axis=0), "ep", split_axis=0, concat_axis=0, tiled=True
        ),
        lax.all_to_all(
            jnp.take(weighted_padded, bwd_index, axis=0),
            "ep",
            split_axis=0,
            concat_axis=0,
            tiled=True,
        ),
    )
    for bit_number in range(bit_count):
        own_bit = own_index >> bit_number & 1
        peer_saved, peer_grads = (
            swapped(shortened(saved_rows), "ep", bit_number).astype(saved_rows.dtype),
            swapped(shortened(grad_rows), "ep", bit_number).astype(grad_rows.dtype),
        )
        saved_rows = arrange(saved_rows, peer_saved, own_bit)
        grad_rows = arrange(grad_rows, peer_grads, own_bit)
    partial_grad = expert_backward(
        saved_rows.reshape(-1, width), grad_rows.reshape(-1, width), joined_cols, down_rows
    )
    partial_grad = partial_grad.reshape(group_size, 1, owners * quarter_slots, width)
    for bit_number in reversed(range(bit_count)):
        own_bit = own_index >> bit_number & 1
        half_rows = partial_grad.shape[0] // 2
        kept_half = lax.dynamic_slice_in_dim(partial_grad, own_bit * half_rows, half_rows, 0)
        sent_half = lax.dynamic_slice_in_dim(partial_grad, (1 - own_bit) * half_rows, half_rows, 0)
        partial_grad = jnp.concatenate([kept_half, swapped(sent_half, "ep", bit_number)], axis=1)
    summed_grad = jnp.sum(partial_grad, axis=(0, 1), dtype=jnp.float32).astype(jnp.bfloat16)
    returned_grad = lax.all_to_all(
        summed_grad.reshape(owners, quarter_slots, width),
        "ep",
        split_axis=0,
        concat_axis=0,
        tiled=True,
    ).reshape(-1, width)
    grad_slot = (
        bwd_chosen * group_size + bwd_rank % group_size
    ) * quarter_slots + bwd_rank // group_size
    bwd_expert = jnp.take(returned_grad, grad_slot, axis=0).astype(jnp.float32)
    fwd_section = (fwd_tokens.astype(jnp.float32) + fwd_weight[:, None] * fwd_expert).astype(
        jnp.bfloat16
    )
    grad_section = (grad_tokens.astype(jnp.float32) + bwd_expert).astype(jnp.bfloat16)
    fwd_next = from_behind(fwd_section[None], "pp", 1)
    grad_next = from_behind(grad_section[None], "pp", -1)
    return (fwd_next, grad_next)


BASE_ROWS = 16
CUTS = 4
COLUMNS = 512
ROWS_BYTES = 2
VMEM_BYTES = 44 << 20
PACK_BYTES = 60 << 20


def transposed_dot(left, right):
    return lax.dot_general(left, right, contract, preferred_element_type=jnp.float32)


def plain_dot(left, right):
    return jnp.dot(left, right, preferred_element_type=jnp.float32)


def slot_masks(ids_row, me, experts):
    tokens = ids_row.shape[1]
    wanted = lax.broadcasted_iota(jnp.int32, (experts, tokens), 0) == ids_row
    chosen = jnp.where(wanted, 1.0, 0.0)
    earlier = jnp.where(
        lax.broadcasted_iota(jnp.int32, (tokens, tokens), 0)
        < lax.broadcasted_iota(jnp.int32, (tokens, tokens), 1),
        1.0,
        0.0,
    )
    before = plain_dot(chosen.astype(jnp.bfloat16), earlier.astype(jnp.bfloat16))
    rank = jnp.sum(before * chosen, axis=0, keepdims=True).astype(jnp.int32)
    row = lax.broadcasted_iota(jnp.int32, (experts * BASE_ROWS, tokens), 0)
    mine = ids_row == ((row // BASE_ROWS) ^ me)
    place = row % BASE_ROWS
    base = jnp.where(mine & (rank == place), 1.0, 0.0).astype(jnp.bfloat16)
    extra = mine & (rank == BASE_ROWS + place % CUTS)
    pieces = [
        jnp.where(extra & (place // CUTS == q), 1.0, 0.0).astype(jnp.bfloat16) for q in range(CUTS)
    ]
    return base, pieces


def pack_kernel(joined, count, experts, own_ids_ref, *refs):
    x_refs = refs[:count]
    held_ref, made_ref, sems, out_sems, ids_ref, ids_sem = refs[-6:]
    refs = refs[:-2]
    ids_copy = pltpu.make_async_copy(own_ids_ref, ids_ref, ids_sem)
    ids_copy.start()
    copies = [pltpu.make_async_copy(x_refs[n], held_ref.at[n], sems.at[n]) for n in range(count)]
    for copy in copies:
        copy.start()
    width = held_ref.shape[2]
    piece = width // CUTS
    first = 0 if joined else lax.axis_index("ep")
    ids_copy.wait()
    base, pieces = slot_masks(ids_ref[...], first, experts)
    for n, copy in enumerate(copies):
        rows = slice(n * BASE_ROWS, (n + 1) * BASE_ROWS)
        copy.wait()
        extra = 0.0
        for q in range(CUTS):
            columns = slice(q * piece, (q + 1) * piece)
            part = held_ref[n, :, columns]
            packed = plain_dot(base, part).astype(jnp.bfloat16)
            extra = extra + plain_dot(pieces[q], part)
            for k in range(experts):
                made_ref[k, rows, columns] = packed[k * BASE_ROWS : (k + 1) * BASE_ROWS]
        extra = extra.astype(jnp.bfloat16)
        for k in range(experts):
            made_ref[k, rows, width:] = extra[k * BASE_ROWS : (k + 1) * BASE_ROWS]
    if joined:
        copies = [pltpu.make_async_copy(made_ref, refs[-5], out_sems.at[0])]
    else:
        out_refs = refs[-4 - experts : -4]
        copies = [
            pltpu.make_async_copy(made_ref.at[k], out_refs[k], out_sems.at[k]) for k in range(experts)
        ]
    for copy in copies:
        copy.start()
    for copy in copies:
        copy.wait()


def unpack_kernel(order, ids_ref, *refs):
    me = lax.axis_index("ep")
    experts = len(order)
    message_refs = [refs[order.index(k)] for k in range(experts)]
    out_ref, made_ref, sems = refs[experts:]
    width = out_ref.shape[1]
    sent = []
    piece = width // CUTS
    base, pieces = slot_masks(ids_ref[...], me, experts)
    from_rows = (((0,), (0,)), ((), ()))
    extra = jnp.concatenate([ref[:, width:] for ref in message_refs], axis=0)
    for q in range(CUTS):
        columns = slice(q * piece, (q + 1) * piece)
        rows = jnp.concatenate([ref[:, columns] for ref in message_refs], axis=0)
        total = lax.dot_general(base, rows, from_rows, preferred_element_type=jnp.float32)
        total = total + lax.dot_general(
            pieces[q], extra, from_rows, preferred_element_type=jnp.float32
        )
        made_ref[:, columns] = total.astype(jnp.bfloat16)
        sent.append(
            pltpu.make_async_copy(made_ref.at[:, columns], out_ref.at[:, columns], sems.at[q])
        )
        sent[q].start()
    for copy in sent:
        copy.wait()


def piece_places(experts, q):
    shape = (experts * CUTS, experts * BASE_ROWS)
    slot = lax.broadcasted_iota(jnp.int32, shape, 0)
    row = lax.broadcasted_iota(jnp.int32, shape, 1)
    same = (slot // CUTS == row // BASE_ROWS) & (row % BASE_ROWS == q * CUTS + slot % CUTS)
    return jnp.where(same, 1.0, 0.0).astype(jnp.bfloat16)


def message_copies(message_refs, place, rows_ref, extra_ref, sems):
    width = rows_ref.shape[1]
    taken = slice(place * BASE_ROWS, (place + 1) * BASE_ROWS)
    copies = []
    for k, ref in enumerate(message_refs):
        rows = slice(k * BASE_ROWS, (k + 1) * BASE_ROWS)
        parts = ((ref.at[taken, :width], rows_ref), (ref.at[taken, width:], extra_ref))
        for n, (source, target) in enumerate(parts):
            copies.append(pltpu.make_async_copy(source, target.at[rows, :], sems.at[n, k]))
    for copy in copies:
        copy.start()
    return copies


def spread(copies, rows_ref, extra_ref):
    width = rows_ref.shape[1]
    piece = width // CUTS
    experts = extra_ref.shape[0] // BASE_ROWS
    for copy in copies:
        copy.wait()
    for q in range(CUTS):
        picked = plain_dot(piece_places(experts, q), extra_ref[...])
        columns = slice(q * piece, (q + 1) * piece)
        rows_ref[experts * BASE_ROWS :, columns] = picked.astype(jnp.bfloat16)


def collect(rows_ref, extra_ref, message_refs, sems):
    experts = len(message_refs)
    width = rows_ref.shape[1]
    piece = width // CUTS
    first = experts * BASE_ROWS
    from_rows = (((0,), (0,)), ((), ()))
    extra = 0.0
    for q in range(CUTS):
        extra = extra + lax.dot_general(
            piece_places(experts, q),
            rows_ref[first:, q * piece : (q + 1) * piece],
            from_rows,
            preferred_element_type=jnp.float32,
        )
    extra_ref[...] = extra.astype(jnp.bfloat16)
    copies = []
    for k, ref in enumerate(message_refs):
        rows = slice(k * BASE_ROWS, (k + 1) * BASE_ROWS)
        parts = ((rows_ref, ref.at[:, :width]), (extra_ref, ref.at[:, width:]))
        for n, (source, target) in enumerate(parts):
            copies.append(pltpu.make_async_copy(source.at[rows, :], target, sems.at[n, k]))
    for copy in copies:
        copy.start()
    for copy in copies:
        copy.wait()


def column_loop(width, step, body):
    for n in range(width // step):
        body(pl.ds(n * step, step))


def row_weight(rows_ref, router_ref):
    row_count, width = rows_ref.shape
    experts = router_ref.shape[0]
    own = lax.broadcasted_iota(jnp.int32, (experts, 128), 0) == lax.axis_index("ep")

    def add(n, total):
        lanes = pl.ds(pl.multiple_of(n * 128, 128), 128)
        centroid = jnp.sum(jnp.where(own, router_ref[:, lanes], 0.0), axis=0, keepdims=True)
        return total + rows_ref[:, lanes].astype(jnp.float32) * centroid

    total = lax.fori_loop(0, width // 128, add, jnp.zeros((row_count, 128), jnp.float32), unroll=4)
    return route_scale * jax.nn.sigmoid(jnp.sum(total, axis=1, keepdims=True))


def weight_copies(weight_refs, held_refs, sems):
    gate_ref, up_ref, down_ref = weight_refs
    steps = sems.shape[1]
    part = gate_ref.shape[1] // steps

    def copies(j):
        units = pl.ds(pl.multiple_of(j * part, part), part)
        places = ((slice(None), units), (slice(None), units), (units, slice(None)))
        return [
            pltpu.make_async_copy(source.at[place], held.at[place], sems.at[n, j])
            for n, (source, held, place) in enumerate(zip(weight_refs, held_refs, places))
        ]

    for j in range(steps):
        for copy in copies(j):
            copy.start()

    def wait(j):
        for copy in copies(j):
            copy.wait()

    return wait


def unit_loop(sems, units, body):
    steps = sems.shape[1]
    part = units // steps

    for j in range(steps):
        body(j, pl.ds(j * part, part))


def forward_kernel(experts, waited, router_ref, *refs):
    me = lax.axis_index("ep")
    weight_refs, message_refs = refs[:3], [refs[3].at[me ^ k] for k in range(experts)]
    refs = refs[4 + waited :]
    out_refs = refs[:experts]
    rows_ref, gate_ref, up_ref, down_ref, sems, extra_ref, message_sems, total_ref = refs[experts:]
    arriving = message_copies(message_refs, 0, rows_ref, extra_ref, message_sems)
    wait = weight_copies(weight_refs, (gate_ref, up_ref, down_ref), sems)
    spread(arriving, rows_ref, extra_ref)
    weight = row_weight(rows_ref, router_ref)

    def project(j, units):
        wait(j)
        gate_proj = plain_dot(rows_ref[...], gate_ref[:, units])
        up_proj = plain_dot(rows_ref[...], up_ref[:, units])
        hidden = (gate_proj * jax.nn.sigmoid(gate_proj) * up_proj).astype(jnp.bfloat16)
        part = plain_dot(hidden, down_ref[units, :])
        total_ref[...] = part if j == 0 else total_ref[...] + part

    unit_loop(sems, gate_ref.shape[1], project)
    expert = total_ref[...].astype(jnp.bfloat16).astype(jnp.float32)
    section = rows_ref[...].astype(jnp.float32) + weight * expert
    rows_ref[...] = section.astype(jnp.bfloat16)
    collect(rows_ref, extra_ref, out_refs, message_sems)


def backward_kernel(order, experts, waited, router_ref, *refs):
    weight_refs = refs[:3]
    message_refs = [refs[3 + order.index(k)] for k in range(experts)]
    refs = refs[3 + experts + waited :]
    out_refs = refs[:experts]
    (
        rows_ref,
        gate_ref,
        up_ref,
        down_ref,
        sems,
        extra_ref,
        message_sems,
        d_gate_ref,
        d_up_ref,
        grads_ref,
        weighted_ref,
        grads_extra_ref,
        grad_sems,
    ) = refs[experts:]
    arriving = message_copies(message_refs, 0, rows_ref, extra_ref, message_sems)
    arriving_grads = message_copies(message_refs, 1, grads_ref, grads_extra_ref, grad_sems)
    wait = weight_copies(weight_refs, (gate_ref, up_ref, down_ref), sems)
    spread(arriving, rows_ref, extra_ref)
    spread(arriving_grads, grads_ref, grads_extra_ref)
    weight = row_weight(rows_ref, router_ref)

    def weigh(columns):
        weighted = weight * grads_ref[:, columns].astype(jnp.float32)
        weighted_ref[:, columns] = weighted.astype(jnp.bfloat16)

    def project(j, units):
        wait(j)
        gate_proj = plain_dot(rows_ref[...], gate_ref[:, units])
        up_proj = plain_dot(rows_ref[...], up_ref[:, units])
        d_hidden = transposed_dot(weighted_ref[...], down_ref[units, :])
        sigmoid_gate = jax.nn.sigmoid(gate_proj)
        d_gate = d_hidden * up_proj * sigmoid_gate * (1.0 + gate_proj * (1.0 - sigmoid_gate))
        d_up = d_hidden * gate_proj * sigmoid_gate
        d_gate_ref[:, units] = d_gate.astype(jnp.bfloat16)
        d_up_ref[:, units] = d_up.astype(jnp.bfloat16)

    def finish(columns):
        total = transposed_dot(d_gate_ref[...], gate_ref[columns, :])
        total = total + transposed_dot(d_up_ref[...], up_ref[columns, :])
        expert = total.astype(jnp.bfloat16).astype(jnp.float32)
        section = grads_ref[:, columns].astype(jnp.float32) + expert
        rows_ref[:, columns] = section.astype(jnp.bfloat16)

    column_loop(rows_ref.shape[1], COLUMNS, weigh)
    unit_loop(sems, d_gate_ref.shape[1], project)
    column_loop(rows_ref.shape[1], COLUMNS, finish)
    collect(rows_ref, extra_ref, out_refs, message_sems)


def pack(ids_row, sources, experts, joined, after=()):
    tokens, width = sources[0].shape
    dtype = sources[0].dtype
    count = len(sources)
    message = (count * BASE_ROWS, width + width // CUTS)
    slots = count * experts * BASE_ROWS
    anywhere = pl.BlockSpec(memory_space=pl.ANY)
    shapes = [(experts, *message)] if joined else [message] * experts
    return pl.pallas_call(
        functools.partial(pack_kernel, joined, count, experts),
        in_specs=[anywhere] * (1 + count + len(after)),
        out_specs=[anywhere] * len(shapes),
        out_shape=[jax.ShapeDtypeStruct(shape, dtype) for shape in shapes],
        scratch_shapes=[
            pltpu.VMEM((count, tokens, width), dtype),
            pltpu.VMEM((experts, *message), dtype),
            pltpu.SemaphoreType.DMA((count,)),
            pltpu.SemaphoreType.DMA((experts,)),
            pltpu.VMEM(ids_row.shape, ids_row.dtype),
            pltpu.SemaphoreType.DMA(()),
        ],
        compiler_params=pltpu.CompilerParams(vmem_limit_bytes=PACK_BYTES),
        cost_estimate=pl.CostEstimate(
            flops=4 * slots * tokens * width,
            bytes_accessed=2 * ROWS_BYTES * slots * width,
            transcendentals=0,
        ),
        name="pack",
    )(ids_row, *sources, *after)


def unpack(ids_row, messages, order):
    experts = len(order)
    tokens = ids_row.shape[1]
    width = messages[0].shape[1] * CUTS // (CUTS + 1)
    slots = experts * BASE_ROWS
    return pl.pallas_call(
        functools.partial(unpack_kernel, order),
        out_specs=pl.BlockSpec(memory_space=pl.ANY),
        out_shape=jax.ShapeDtypeStruct((tokens, width), messages[0].dtype),
        scratch_shapes=[
            pltpu.VMEM((tokens, width), messages[0].dtype),
            pltpu.SemaphoreType.DMA((CUTS,)),
        ],
        compiler_params=pltpu.CompilerParams(vmem_limit_bytes=16 << 20),
        cost_estimate=pl.CostEstimate(
            flops=4 * slots * tokens * width,
            bytes_accessed=2 * ROWS_BYTES * slots * width,
            transcendentals=0,
        ),
        name="unpack",
    )(ids_row, *[messages[k] for k in order])


def expert_call(
    kernel, name, router_rows, gate_cols, up_cols, down_rows, messages, experts, products, after
):
    width, units = gate_cols.shape
    row_count = experts * (BASE_ROWS + CUTS)
    steps = 4 if units % 512 == 0 else 1
    result_shape = (BASE_ROWS, messages[0].shape[-1])
    in_vmem = pl.BlockSpec(memory_space=pltpu.VMEM)
    anywhere = pl.BlockSpec(memory_space=pl.ANY)
    rows_scratch = pltpu.VMEM((row_count, width), jnp.bfloat16)
    message_scratch = [
        pltpu.VMEM((experts * BASE_ROWS, width // CUTS), jnp.bfloat16),
        pltpu.SemaphoreType.DMA((2, experts)),
    ]
    if products > 3:
        own_scratch = [pltpu.VMEM((row_count, units), jnp.bfloat16)] * 2
        own_scratch += [rows_scratch] * 2 + message_scratch
    else:
        own_scratch = [pltpu.VMEM((row_count, width), jnp.float32)]
    return pl.pallas_call(
        functools.partial(kernel, experts, len(after)),
        in_specs=[in_vmem] + [anywhere] * (3 + len(messages) + len(after)),
        out_specs=[anywhere] * experts,
        out_shape=[jax.ShapeDtypeStruct(result_shape, messages[0].dtype)] * experts,
        scratch_shapes=[
            rows_scratch,
            pltpu.VMEM((width, units), jnp.bfloat16),
            pltpu.VMEM((width, units), jnp.bfloat16),
            pltpu.VMEM((units, width), jnp.bfloat16),
            pltpu.SemaphoreType.DMA((3, steps)),
            *message_scratch,
            *own_scratch,
        ],
        compiler_params=pltpu.CompilerParams(vmem_limit_bytes=VMEM_BYTES),
        cost_estimate=pl.CostEstimate(
            flops=2 * products * row_count * width * units,
            bytes_accessed=3 * ROWS_BYTES * width * units,
            transcendentals=row_count * units,
        ),
        name=name,
    )(router_rows, gate_cols, up_cols, down_rows, *messages, *after)


def exchanged(messages, order):
    experts = len(messages)
    arrived = list(messages)
    for k in order:
        arrived[k] = lax.ppermute(messages[k], "ep", [(i, i ^ k) for i in range(experts)])
    return arrived


def returned(messages, order, steps):
    sections, experts = lax.axis_size("pp"), len(messages)
    back = list(messages)
    for k in order:
        pairs = [
            (p * experts + e, (p + steps) % sections * experts + (e ^ k))
            for p in range(sections)
            for e in range(experts)
        ]
        back[k] = lax.ppermute(messages[k], ("pp", "ep"), pairs)
    return back


def per_device_whole(fwd_in, fwd_ids, saved_in, bwd_ids, grad_in, router, w_gate, w_up, w_down):
    experts = router.shape[-1]
    token_count = fwd_in.shape[1]
    router_rows = router[0].T
    weights = (w_gate[0], w_up[0], w_down[0])
    fwd_row, bwd_row = fwd_ids.reshape(1, token_count), bwd_ids.reshape(1, token_count)
    near, far = list(range(1, experts // 2)), list(range(experts // 2, experts))
    fwd_packed = pack(fwd_row, [fwd_in[0]], experts, True)
    fwd_rows = lax.all_to_all(fwd_packed[0], "ep", split_axis=0, concat_axis=0, tiled=True)
    all_ids = lax.all_gather(jnp.concatenate([fwd_row, bwd_row], axis=0), "pp")
    section, sections = lax.axis_index("pp"), lax.axis_size("pp")
    fwd_row_next = lax.dynamic_index_in_dim(all_ids, (section + sections - 1) % sections, 0, False)[:1]
    bwd_row_next = lax.dynamic_index_in_dim(all_ids, (section + 1) % sections, 0, False)[1:]
    after = [fwd_packed[0]]
    bwd_packed = pack(bwd_row, [saved_in[0], grad_in[0]], experts, False, after)
    order = [0, *near, *far]
    bwd_rows = exchanged(bwd_packed, order[1:])
    after = [bwd_rows[k] for k in near] + [fwd_row_next, bwd_row_next]
    fwd_out = expert_call(
        forward_kernel, "forward", router_rows, *weights, [fwd_rows], experts, 3, after
    )
    fwd_back = returned(fwd_out, range(experts), 1)
    after = [fwd_back[k] for k in near + [0]]
    bwd_out = expert_call(
        functools.partial(backward_kernel, order), "backward", router_rows, *weights, [bwd_rows[k] for k in order], experts, 5, after
    )
    bwd_back = returned(bwd_out, range(experts), -1)
    fwd_next = unpack(fwd_row_next, fwd_back, near + [0] + far)
    grad_next = unpack(bwd_row_next, bwd_back, far[:1] + near + far[1:] + [0])
    return (fwd_next[None], grad_next[None])


def solution(mesh):
    in_specs = (
        P("pp", "ep", None),
        P("pp", "ep", None),
        P("pp", "ep", None),
        P("pp", "ep", None),
        P("pp", "ep", None),
        P("pp", None, None),
        P("pp", None, "ep"),
        P("pp", None, "ep"),
        P("pp", "ep", None),
    )
    out_specs = (P("pp", "ep", None), P("pp", "ep", None))

    def layer(*arrays):
        token_count = arrays[0].shape[1] // mesh.shape["ep"]
        width = arrays[0].shape[2]
        experts = arrays[5].shape[-1]
        whole = (
            mesh.shape["ep"] == experts
            and experts & (experts - 1) == 0
            and 5 * token_count // (4 * experts) == BASE_ROWS + CUTS
            and width % (128 * CUTS) == 0
        )
        return jax.shard_map(
            per_device_whole if whole else per_device,
            mesh=mesh,
            in_specs=in_specs,
            out_specs=out_specs,
            check_vma=False,
        )(*arrays)

    return layer
```

```python
import functools

import jax
import jax.numpy as jnp
from jax import lax
from jax.experimental import pallas as pl
from jax.experimental.pallas import tpu as pltpu
from jax.sharding import PartitionSpec as P

route_scale = 2.5
contract = (((1,), (1,)), ((), ()))


def shortened(value):

    def short(part):
        return part.astype(jnp.bfloat16) if part.dtype == jnp.float32 else part

    return jax.tree.map(short, value)


def swapped(value, axis, distance):
    return lax.ppermute(value, axis, [(i, i ^ 1 << distance) for i in range(lax.axis_size(axis))])


def from_behind(value, axis, steps):
    count = lax.axis_size(axis)
    pairs = [(source, (source + steps) % count) for source in range(count)]
    return lax.ppermute(value, axis, pairs)


def order_slots(chosen, experts, capacity):
    token_count = chosen.shape[0]
    onehot = (chosen[:, None] == jnp.arange(experts, dtype=jnp.int32)[None, :]).astype(jnp.int32)
    before = jnp.cumsum(onehot, axis=0) - onehot
    ranking = jnp.sum(before * onehot, axis=1)
    slot_table = jnp.full((experts * capacity,), token_count, jnp.int32)
    slot_table = slot_table.at[chosen * capacity + ranking].set(
        jnp.arange(token_count, dtype=jnp.int32)
    )
    return (onehot, ranking, slot_table)


def routing_weight(tokens, router, onehot):
    logits = jnp.dot(tokens.astype(jnp.float32), router, precision=lax.Precision.HIGHEST)
    picked = jnp.sum(jnp.where(onehot > 0, logits, 0.0), axis=1)
    return route_scale * jax.nn.sigmoid(picked)


def with_zero_row(tokens):
    return jnp.concatenate([tokens, jnp.zeros((1, tokens.shape[1]), tokens.dtype)], axis=0)


def expert_forward(row_block, gate_cols, up_cols, down_rows):
    gate_proj = jnp.dot(row_block, gate_cols, preferred_element_type=jnp.float32)
    up_proj = jnp.dot(row_block, up_cols, preferred_element_type=jnp.float32)
    hidden = (gate_proj * jax.nn.sigmoid(gate_proj) * up_proj).astype(jnp.bfloat16)
    return jnp.dot(hidden, down_rows, preferred_element_type=jnp.float32).astype(jnp.bfloat16)


def expert_backward(row_block, row_grads, joined_cols, down_rows):
    unit_count = down_rows.shape[0]
    both_proj = jnp.dot(row_block, joined_cols, preferred_element_type=jnp.float32)
    gate_proj = both_proj[:, :unit_count]
    up_proj = both_proj[:, unit_count:]
    d_hidden = lax.dot_general(row_grads, down_rows, contract, preferred_element_type=jnp.float32)
    sigmoid_gate = jax.nn.sigmoid(gate_proj)
    d_gate = (d_hidden * up_proj * sigmoid_gate * (1.0 + gate_proj * (1.0 - sigmoid_gate))).astype(
        jnp.bfloat16
    )
    d_up = (d_hidden * gate_proj * sigmoid_gate).astype(jnp.bfloat16)
    d_joined = jnp.concatenate([d_gate, d_up], axis=1)
    partial_sum = lax.dot_general(
        d_joined, joined_cols, contract, preferred_element_type=jnp.float32
    )
    return partial_sum.astype(jnp.bfloat16)


def arrange(own_rows, peer_rows, own_bit):
    return jnp.where(
        own_bit == 0, jnp.stack([own_rows, peer_rows]), jnp.stack([peer_rows, own_rows])
    )


def per_device(fwd_in, fwd_ids, saved_in, bwd_ids, grad_in, router, w_gate, w_up, w_down):
    experts = router.shape[-1]
    owners = lax.axis_size("ep")
    group_size = owners // experts
    bit_count = group_size.bit_length() - 1
    own_index = lax.axis_index("ep")
    token_count = fwd_in.shape[1]
    width = fwd_in.shape[2]
    capacity = group_size * max(1, 5 * token_count // (4 * experts * group_size))
    quarter_slots = capacity // group_size
    router_section = router[0]
    gate_cols = w_gate[0]
    up_cols = w_up[0]
    down_rows = w_down[0]
    joined_cols = jnp.concatenate([gate_cols, up_cols], axis=1)
    fwd_tokens = fwd_in[0]
    fwd_chosen = fwd_ids[0, :, 0]
    fwd_onehot, fwd_rank, fwd_table = order_slots(fwd_chosen, experts, capacity)
    fwd_weight = routing_weight(fwd_tokens, router_section, fwd_onehot)
    fwd_padded = with_zero_row(fwd_tokens)
    saved_tokens = saved_in[0]
    bwd_chosen = bwd_ids[0, :, 0]
    grad_tokens = grad_in[0]
    bwd_onehot, bwd_rank, bwd_table = order_slots(bwd_chosen, experts, capacity)
    bwd_weight = routing_weight(saved_tokens, router_section, bwd_onehot)
    weighted = (bwd_weight[:, None] * grad_tokens.astype(jnp.float32)).astype(jnp.bfloat16)
    saved_padded = with_zero_row(saved_tokens)
    weighted_padded = with_zero_row(weighted)
    fwd_index = (
        fwd_table.reshape(experts, quarter_slots, group_size)
        .transpose(0, 2, 1)
        .reshape(owners, quarter_slots)
    )
    gathered = lax.all_to_all(
        jnp.take(fwd_padded, fwd_index, axis=0), "ep", split_axis=0, concat_axis=0, tiled=True
    )
    for bit_number in range(bit_count):
        own_bit = own_index >> bit_number & 1
        peer_rows = swapped(shortened(gathered), "ep", bit_number).astype(gathered.dtype)
        gathered = arrange(gathered, peer_rows, own_bit)
    partial_out = expert_forward(gathered.reshape(-1, width), gate_cols, up_cols, down_rows)
    partial_out = partial_out.reshape(group_size, 1, owners * quarter_slots, width)
    for bit_number in reversed(range(bit_count)):
        own_bit = own_index >> bit_number & 1
        half_rows = partial_out.shape[0] // 2
        kept_half = lax.dynamic_slice_in_dim(partial_out, own_bit * half_rows, half_rows, 0)
        sent_half = lax.dynamic_slice_in_dim(partial_out, (1 - own_bit) * half_rows, half_rows, 0)
        partial_out = jnp.concatenate([kept_half, swapped(sent_half, "ep", bit_number)], axis=1)
    summed = jnp.sum(partial_out, axis=(0, 1), dtype=jnp.float32).astype(jnp.bfloat16)
    returned = lax.all_to_all(
        summed.reshape(owners, quarter_slots, width), "ep", split_axis=0, concat_axis=0, tiled=True
    ).reshape(-1, width)
    source_slot = (
        fwd_chosen * group_size + fwd_rank % group_size
    ) * quarter_slots + fwd_rank // group_size
    fwd_expert = jnp.take(returned, source_slot, axis=0).astype(jnp.float32)
    bwd_index = (
        bwd_table.reshape(experts, quarter_slots, group_size)
        .transpose(0, 2, 1)
        .reshape(owners, quarter_slots)
    )
    saved_rows, grad_rows = (
        lax.all_to_all(
            jnp.take(saved_padded, bwd_index, axis=0), "ep", split_axis=0, concat_axis=0, tiled=True
        ),
        lax.all_to_all(
            jnp.take(weighted_padded, bwd_index, axis=0),
            "ep",
            split_axis=0,
            concat_axis=0,
            tiled=True,
        ),
    )
    for bit_number in range(bit_count):
        own_bit = own_index >> bit_number & 1
        peer_saved, peer_grads = (
            swapped(shortened(saved_rows), "ep", bit_number).astype(saved_rows.dtype),
            swapped(shortened(grad_rows), "ep", bit_number).astype(grad_rows.dtype),
        )
        saved_rows = arrange(saved_rows, peer_saved, own_bit)
        grad_rows = arrange(grad_rows, peer_grads, own_bit)
    partial_grad = expert_backward(
        saved_rows.reshape(-1, width), grad_rows.reshape(-1, width), joined_cols, down_rows
    )
    partial_grad = partial_grad.reshape(group_size, 1, owners * quarter_slots, width)
    for bit_number in reversed(range(bit_count)):
        own_bit = own_index >> bit_number & 1
        half_rows = partial_grad.shape[0] // 2
        kept_half = lax.dynamic_slice_in_dim(partial_grad, own_bit * half_rows, half_rows, 0)
        sent_half = lax.dynamic_slice_in_dim(partial_grad, (1 - own_bit) * half_rows, half_rows, 0)
        partial_grad = jnp.concatenate([kept_half, swapped(sent_half, "ep", bit_number)], axis=1)
    summed_grad = jnp.sum(partial_grad, axis=(0, 1), dtype=jnp.float32).astype(jnp.bfloat16)
    returned_grad = lax.all_to_all(
        summed_grad.reshape(owners, quarter_slots, width),
        "ep",
        split_axis=0,
        concat_axis=0,
        tiled=True,
    ).reshape(-1, width)
    grad_slot = (
        bwd_chosen * group_size + bwd_rank % group_size
    ) * quarter_slots + bwd_rank // group_size
    bwd_expert = jnp.take(returned_grad, grad_slot, axis=0).astype(jnp.float32)
    fwd_section = (fwd_tokens.astype(jnp.float32) + fwd_weight[:, None] * fwd_expert).astype(
        jnp.bfloat16
    )
    grad_section = (grad_tokens.astype(jnp.float32) + bwd_expert).astype(jnp.bfloat16)
    fwd_next = from_behind(fwd_section[None], "pp", 1)
    grad_next = from_behind(grad_section[None], "pp", -1)
    return (fwd_next, grad_next)


BASE_ROWS = 16
CUTS = 4
COLUMNS = 512
ROWS_BYTES = 2
VMEM_BYTES = 44 << 20
PACK_BYTES = 60 << 20


def transposed_dot(left, right):
    return lax.dot_general(left, right, contract, preferred_element_type=jnp.float32)


def plain_dot(left, right):
    return jnp.dot(left, right, preferred_element_type=jnp.float32)


def slot_masks(ids_row, me, experts):
    tokens = ids_row.shape[1]
    wanted = lax.broadcasted_iota(jnp.int32, (experts, tokens), 0) == ids_row
    chosen = jnp.where(wanted, 1.0, 0.0)
    earlier = jnp.where(
        lax.broadcasted_iota(jnp.int32, (tokens, tokens), 0)
        < lax.broadcasted_iota(jnp.int32, (tokens, tokens), 1),
        1.0,
        0.0,
    )
    before = plain_dot(chosen.astype(jnp.bfloat16), earlier.astype(jnp.bfloat16))
    rank = jnp.sum(before * chosen, axis=0, keepdims=True).astype(jnp.int32)
    row = lax.broadcasted_iota(jnp.int32, (experts * BASE_ROWS, tokens), 0)
    mine = ids_row == ((row // BASE_ROWS) ^ me)
    place = row % BASE_ROWS
    base = jnp.where(mine & (rank == place), 1.0, 0.0).astype(jnp.bfloat16)
    extra = mine & (rank == BASE_ROWS + place % CUTS)
    pieces = [
        jnp.where(extra & (place // CUTS == q), 1.0, 0.0).astype(jnp.bfloat16) for q in range(CUTS)
    ]
    return base, pieces


def pack_kernel(joined, count, experts, own_ids_ref, *refs):
    x_refs = refs[:count]
    held_ref, made_ref, sems, out_sems, ids_ref, ids_sem = refs[-6:]
    refs = refs[:-2]
    ids_copy = pltpu.make_async_copy(own_ids_ref, ids_ref, ids_sem)
    ids_copy.start()
    copies = [pltpu.make_async_copy(x_refs[n], held_ref.at[n], sems.at[n]) for n in range(count)]
    for copy in copies:
        copy.start()
    width = held_ref.shape[2]
    piece = width // CUTS
    first = 0 if joined else lax.axis_index("ep")
    ids_copy.wait()
    base, pieces = slot_masks(ids_ref[...], first, experts)
    for n, copy in enumerate(copies):
        rows = slice(n * BASE_ROWS, (n + 1) * BASE_ROWS)
        copy.wait()
        extra = 0.0
        for q in range(CUTS):
            columns = slice(q * piece, (q + 1) * piece)
            part = held_ref[n, :, columns]
            packed = plain_dot(base, part).astype(jnp.bfloat16)
            extra = extra + plain_dot(pieces[q], part)
            for k in range(experts):
                made_ref[k, rows, columns] = packed[k * BASE_ROWS : (k + 1) * BASE_ROWS]
        extra = extra.astype(jnp.bfloat16)
        for k in range(experts):
            made_ref[k, rows, width:] = extra[k * BASE_ROWS : (k + 1) * BASE_ROWS]
    if joined:
        copies = [pltpu.make_async_copy(made_ref, refs[-5], out_sems.at[0])]
    else:
        out_refs = refs[-4 - experts : -4]
        copies = [
            pltpu.make_async_copy(made_ref.at[k], out_refs[k], out_sems.at[k]) for k in range(experts)
        ]
    for copy in copies:
        copy.start()
    for copy in copies:
        copy.wait()


def unpack_kernel(order, ids_ref, *refs):
    me = lax.axis_index("ep")
    experts = len(order)
    message_refs = [refs[order.index(k)] for k in range(experts)]
    out_ref, made_ref, sems = refs[experts:]
    width = out_ref.shape[1]
    sent = []
    piece = width // CUTS
    base, pieces = slot_masks(ids_ref[...], me, experts)
    from_rows = (((0,), (0,)), ((), ()))
    extra = jnp.concatenate([ref[:, width:] for ref in message_refs], axis=0)
    for q in range(CUTS):
        columns = slice(q * piece, (q + 1) * piece)
        rows = jnp.concatenate([ref[:, columns] for ref in message_refs], axis=0)
        total = lax.dot_general(base, rows, from_rows, preferred_element_type=jnp.float32)
        total = total + lax.dot_general(
            pieces[q], extra, from_rows, preferred_element_type=jnp.float32
        )
        made_ref[:, columns] = total.astype(jnp.bfloat16)
        sent.append(
            pltpu.make_async_copy(made_ref.at[:, columns], out_ref.at[:, columns], sems.at[q])
        )
        sent[q].start()
    for copy in sent:
        copy.wait()


def piece_places(experts, q):
    shape = (experts * CUTS, experts * BASE_ROWS)
    slot = lax.broadcasted_iota(jnp.int32, shape, 0)
    row = lax.broadcasted_iota(jnp.int32, shape, 1)
    same = (slot // CUTS == row // BASE_ROWS) & (row % BASE_ROWS == q * CUTS + slot % CUTS)
    return jnp.where(same, 1.0, 0.0).astype(jnp.bfloat16)


def message_copies(message_refs, place, rows_ref, extra_ref, sems):
    width = rows_ref.shape[1]
    taken = slice(place * BASE_ROWS, (place + 1) * BASE_ROWS)
    copies = []
    for k, ref in enumerate(message_refs):
        rows = slice(k * BASE_ROWS, (k + 1) * BASE_ROWS)
        parts = ((ref.at[taken, :width], rows_ref), (ref.at[taken, width:], extra_ref))
        for n, (source, target) in enumerate(parts):
            copies.append(pltpu.make_async_copy(source, target.at[rows, :], sems.at[n, k]))
    for copy in copies:
        copy.start()
    return copies


def spread(copies, rows_ref, extra_ref):
    width = rows_ref.shape[1]
    piece = width // CUTS
    experts = extra_ref.shape[0] // BASE_ROWS
    for copy in copies:
        copy.wait()
    for q in range(CUTS):
        picked = plain_dot(piece_places(experts, q), extra_ref[...])
        columns = slice(q * piece, (q + 1) * piece)
        rows_ref[experts * BASE_ROWS :, columns] = picked.astype(jnp.bfloat16)


def collect(rows_ref, extra_ref, message_refs, sems):
    experts = len(message_refs)
    width = rows_ref.shape[1]
    piece = width // CUTS
    first = experts * BASE_ROWS
    from_rows = (((0,), (0,)), ((), ()))
    extra = 0.0
    for q in range(CUTS):
        extra = extra + lax.dot_general(
            piece_places(experts, q),
            rows_ref[first:, q * piece : (q + 1) * piece],
            from_rows,
            preferred_element_type=jnp.float32,
        )
    extra_ref[...] = extra.astype(jnp.bfloat16)
    copies = []
    for k, ref in enumerate(message_refs):
        rows = slice(k * BASE_ROWS, (k + 1) * BASE_ROWS)
        parts = ((rows_ref, ref.at[:, :width]), (extra_ref, ref.at[:, width:]))
        for n, (source, target) in enumerate(parts):
            copies.append(pltpu.make_async_copy(source.at[rows, :], target, sems.at[n, k]))
    for copy in copies:
        copy.start()
    for copy in copies:
        copy.wait()


def column_loop(width, step, body):
    for n in range(width // step):
        body(pl.ds(n * step, step))


def row_weight(rows_ref, router_ref):
    row_count, width = rows_ref.shape
    experts = router_ref.shape[0]
    own = lax.broadcasted_iota(jnp.int32, (experts, 128), 0) == lax.axis_index("ep")

    def add(n, total):
        lanes = pl.ds(pl.multiple_of(n * 128, 128), 128)
        centroid = jnp.sum(jnp.where(own, router_ref[:, lanes], 0.0), axis=0, keepdims=True)
        return total + rows_ref[:, lanes].astype(jnp.float32) * centroid

    total = lax.fori_loop(0, width // 128, add, jnp.zeros((row_count, 128), jnp.float32), unroll=4)
    return route_scale * jax.nn.sigmoid(jnp.sum(total, axis=1, keepdims=True))


def weight_copies(weight_refs, held_refs, sems):
    gate_ref, up_ref, down_ref = weight_refs
    steps = sems.shape[1]
    part = gate_ref.shape[1] // steps

    def copies(j):
        units = pl.ds(pl.multiple_of(j * part, part), part)
        places = ((slice(None), units), (slice(None), units), (units, slice(None)))
        return [
            pltpu.make_async_copy(source.at[place], held.at[place], sems.at[n, j])
            for n, (source, held, place) in enumerate(zip(weight_refs, held_refs, places))
        ]

    for j in range(steps):
        for copy in copies(j):
            copy.start()

    def wait(j):
        for copy in copies(j):
            copy.wait()

    return wait


def unit_loop(sems, units, body):
    steps = sems.shape[1]
    part = units // steps

    for j in range(steps):
        body(j, pl.ds(j * part, part))


def forward_kernel(experts, waited, router_ref, *refs):
    me = lax.axis_index("ep")
    weight_refs, message_refs = refs[:3], [refs[3].at[me ^ k] for k in range(experts)]
    refs = refs[4 + waited :]
    out_refs = refs[:experts]
    rows_ref, gate_ref, up_ref, down_ref, sems, extra_ref, message_sems, total_ref = refs[experts:]
    arriving = message_copies(message_refs, 0, rows_ref, extra_ref, message_sems)
    wait = weight_copies(weight_refs, (gate_ref, up_ref, down_ref), sems)
    spread(arriving, rows_ref, extra_ref)
    weight = row_weight(rows_ref, router_ref)

    def project(j, units):
        wait(j)
        gate_proj = plain_dot(rows_ref[...], gate_ref[:, units])
        up_proj = plain_dot(rows_ref[...], up_ref[:, units])
        hidden = (gate_proj * jax.nn.sigmoid(gate_proj) * up_proj).astype(jnp.bfloat16)
        part = plain_dot(hidden, down_ref[units, :])
        total_ref[...] = part if j == 0 else total_ref[...] + part

    unit_loop(sems, gate_ref.shape[1], project)
    expert = total_ref[...].astype(jnp.bfloat16).astype(jnp.float32)
    section = rows_ref[...].astype(jnp.float32) + weight * expert
    rows_ref[...] = section.astype(jnp.bfloat16)
    collect(rows_ref, extra_ref, out_refs, message_sems)


def backward_kernel(order, experts, waited, router_ref, *refs):
    weight_refs = refs[:3]
    message_refs = [refs[3 + order.index(k)] for k in range(experts)]
    refs = refs[3 + experts + waited :]
    out_refs = refs[:experts]
    (
        rows_ref,
        gate_ref,
        up_ref,
        down_ref,
        sems,
        extra_ref,
        message_sems,
        d_gate_ref,
        d_up_ref,
        grads_ref,
        weighted_ref,
        grads_extra_ref,
        grad_sems,
    ) = refs[experts:]
    arriving = message_copies(message_refs, 0, rows_ref, extra_ref, message_sems)
    arriving_grads = message_copies(message_refs, 1, grads_ref, grads_extra_ref, grad_sems)
    wait = weight_copies(weight_refs, (gate_ref, up_ref, down_ref), sems)
    spread(arriving, rows_ref, extra_ref)
    spread(arriving_grads, grads_ref, grads_extra_ref)
    weight = row_weight(rows_ref, router_ref)

    def weigh(columns):
        weighted = weight * grads_ref[:, columns].astype(jnp.float32)
        weighted_ref[:, columns] = weighted.astype(jnp.bfloat16)

    def project(j, units):
        wait(j)
        gate_proj = plain_dot(rows_ref[...], gate_ref[:, units])
        up_proj = plain_dot(rows_ref[...], up_ref[:, units])
        d_hidden = transposed_dot(weighted_ref[...], down_ref[units, :])
        sigmoid_gate = jax.nn.sigmoid(gate_proj)
        d_gate = d_hidden * up_proj * sigmoid_gate * (1.0 + gate_proj * (1.0 - sigmoid_gate))
        d_up = d_hidden * gate_proj * sigmoid_gate
        d_gate_ref[:, units] = d_gate.astype(jnp.bfloat16)
        d_up_ref[:, units] = d_up.astype(jnp.bfloat16)

    def finish(columns):
        total = transposed_dot(d_gate_ref[...], gate_ref[columns, :])
        total = total + transposed_dot(d_up_ref[...], up_ref[columns, :])
        expert = total.astype(jnp.bfloat16).astype(jnp.float32)
        section = grads_ref[:, columns].astype(jnp.float32) + expert
        rows_ref[:, columns] = section.astype(jnp.bfloat16)

    column_loop(rows_ref.shape[1], COLUMNS, weigh)
    unit_loop(sems, d_gate_ref.shape[1], project)
    column_loop(rows_ref.shape[1], COLUMNS, finish)
    collect(rows_ref, extra_ref, out_refs, message_sems)


def pack(ids_row, sources, experts, joined, after=()):
    tokens, width = sources[0].shape
    dtype = sources[0].dtype
    count = len(sources)
    message = (count * BASE_ROWS, width + width // CUTS)
    slots = count * experts * BASE_ROWS
    anywhere = pl.BlockSpec(memory_space=pl.ANY)
    shapes = [(experts, *message)] if joined else [message] * experts
    return pl.pallas_call(
        functools.partial(pack_kernel, joined, count, experts),
        in_specs=[anywhere] * (1 + count + len(after)),
        out_specs=[anywhere] * len(shapes),
        out_shape=[jax.ShapeDtypeStruct(shape, dtype) for shape in shapes],
        scratch_shapes=[
            pltpu.VMEM((count, tokens, width), dtype),
            pltpu.VMEM((experts, *message), dtype),
            pltpu.SemaphoreType.DMA((count,)),
            pltpu.SemaphoreType.DMA((experts,)),
            pltpu.VMEM(ids_row.shape, ids_row.dtype),
            pltpu.SemaphoreType.DMA(()),
        ],
        compiler_params=pltpu.CompilerParams(vmem_limit_bytes=PACK_BYTES),
        cost_estimate=pl.CostEstimate(
            flops=4 * slots * tokens * width,
            bytes_accessed=2 * ROWS_BYTES * slots * width,
            transcendentals=0,
        ),
        name="pack",
    )(ids_row, *sources, *after)


def unpack(ids_row, messages, order):
    experts = len(order)
    tokens = ids_row.shape[1]
    width = messages[0].shape[1] * CUTS // (CUTS + 1)
    slots = experts * BASE_ROWS
    return pl.pallas_call(
        functools.partial(unpack_kernel, order),
        out_specs=pl.BlockSpec(memory_space=pl.ANY),
        out_shape=jax.ShapeDtypeStruct((tokens, width), messages[0].dtype),
        scratch_shapes=[
            pltpu.VMEM((tokens, width), messages[0].dtype),
            pltpu.SemaphoreType.DMA((CUTS,)),
        ],
        compiler_params=pltpu.CompilerParams(vmem_limit_bytes=16 << 20),
        cost_estimate=pl.CostEstimate(
            flops=4 * slots * tokens * width,
            bytes_accessed=2 * ROWS_BYTES * slots * width,
            transcendentals=0,
        ),
        name="unpack",
    )(ids_row, *[messages[k] for k in order])


def expert_call(
    kernel, name, router_rows, gate_cols, up_cols, down_rows, messages, experts, products, after
):
    width, units = gate_cols.shape
    row_count = experts * (BASE_ROWS + CUTS)
    steps = 4 if units % 512 == 0 else 1
    result_shape = (BASE_ROWS, messages[0].shape[-1])
    in_vmem = pl.BlockSpec(memory_space=pltpu.VMEM)
    anywhere = pl.BlockSpec(memory_space=pl.ANY)
    rows_scratch = pltpu.VMEM((row_count, width), jnp.bfloat16)
    message_scratch = [
        pltpu.VMEM((experts * BASE_ROWS, width // CUTS), jnp.bfloat16),
        pltpu.SemaphoreType.DMA((2, experts)),
    ]
    if products > 3:
        own_scratch = [pltpu.VMEM((row_count, units), jnp.bfloat16)] * 2
        own_scratch += [rows_scratch] * 2 + message_scratch
    else:
        own_scratch = [pltpu.VMEM((row_count, width), jnp.float32)]
    return pl.pallas_call(
        functools.partial(kernel, experts, len(after)),
        in_specs=[in_vmem] + [anywhere] * (3 + len(messages) + len(after)),
        out_specs=[anywhere] * experts,
        out_shape=[jax.ShapeDtypeStruct(result_shape, messages[0].dtype)] * experts,
        scratch_shapes=[
            rows_scratch,
            pltpu.VMEM((width, units), jnp.bfloat16),
            pltpu.VMEM((width, units), jnp.bfloat16),
            pltpu.VMEM((units, width), jnp.bfloat16),
            pltpu.SemaphoreType.DMA((3, steps)),
            *message_scratch,
            *own_scratch,
        ],
        compiler_params=pltpu.CompilerParams(vmem_limit_bytes=VMEM_BYTES),
        cost_estimate=pl.CostEstimate(
            flops=2 * products * row_count * width * units,
            bytes_accessed=3 * ROWS_BYTES * width * units,
            transcendentals=row_count * units,
        ),
        name=name,
    )(router_rows, gate_cols, up_cols, down_rows, *messages, *after)


def exchanged(messages, order):
    experts = len(messages)
    arrived = list(messages)
    for k in order:
        arrived[k] = lax.ppermute(messages[k], "ep", [(i, i ^ k) for i in range(experts)])
    return arrived


def returned(messages, order, steps):
    sections, experts = lax.axis_size("pp"), len(messages)
    back = list(messages)
    for k in order:
        pairs = [
            (p * experts + e, (p + steps) % sections * experts + (e ^ k))
            for p in range(sections)
            for e in range(experts)
        ]
        back[k] = lax.ppermute(messages[k], ("pp", "ep"), pairs)
    return back


def per_device_whole(fwd_in, fwd_ids, saved_in, bwd_ids, grad_in, router, w_gate, w_up, w_down):
    experts = router.shape[-1]
    token_count = fwd_in.shape[1]
    router_rows = router[0].T
    weights = (w_gate[0], w_up[0], w_down[0])
    fwd_row, bwd_row = fwd_ids.reshape(1, token_count), bwd_ids.reshape(1, token_count)
    near, far = list(range(1, experts // 2)), list(range(experts // 2, experts))
    fwd_packed = pack(fwd_row, [fwd_in[0]], experts, True)
    fwd_rows = lax.all_to_all(fwd_packed[0], "ep", split_axis=0, concat_axis=0, tiled=True)
    all_ids = lax.all_gather(jnp.concatenate([fwd_row, bwd_row], axis=0), "pp")
    section, sections = lax.axis_index("pp"), lax.axis_size("pp")
    fwd_row_next = lax.dynamic_index_in_dim(all_ids, (section + sections - 1) % sections, 0, False)[:1]
    bwd_row_next = lax.dynamic_index_in_dim(all_ids, (section + 1) % sections, 0, False)[1:]
    after = [fwd_packed[0]]
    bwd_packed = pack(bwd_row, [saved_in[0], grad_in[0]], experts, False, after)
    order = [0, *near, *far]
    bwd_rows = exchanged(bwd_packed, order[1:])
    after = [bwd_rows[k] for k in near[:1]] + [fwd_row_next, bwd_row_next]
    fwd_out = expert_call(
        forward_kernel, "forward", router_rows, *weights, [fwd_rows], experts, 3, after
    )
    fwd_back = returned(fwd_out, range(experts), 1)
    after = [fwd_back[k] for k in near + [0]]
    bwd_out = expert_call(
        functools.partial(backward_kernel, order), "backward", router_rows, *weights, [bwd_rows[k] for k in order], experts, 5, after
    )
    bwd_back = returned(bwd_out, range(experts), -1)
    fwd_next = unpack(fwd_row_next, fwd_back, near + [0] + far)
    grad_next = unpack(bwd_row_next, bwd_back, far[:1] + near + far[1:2] + [0] + far[2:])
    return (fwd_next[None], grad_next[None])


def solution(mesh):
    in_specs = (
        P("pp", "ep", None),
        P("pp", "ep", None),
        P("pp", "ep", None),
        P("pp", "ep", None),
        P("pp", "ep", None),
        P("pp", None, None),
        P("pp", None, "ep"),
        P("pp", None, "ep"),
        P("pp", "ep", None),
    )
    out_specs = (P("pp", "ep", None), P("pp", "ep", None))

    def layer(*arrays):
        token_count = arrays[0].shape[1] // mesh.shape["ep"]
        width = arrays[0].shape[2]
        experts = arrays[5].shape[-1]
        whole = (
            mesh.shape["ep"] == experts
            and experts & (experts - 1) == 0
            and 5 * token_count // (4 * experts) == BASE_ROWS + CUTS
            and width % (128 * CUTS) == 0
        )
        return jax.shard_map(
            per_device_whole if whole else per_device,
            mesh=mesh,
            in_specs=in_specs,
            out_specs=out_specs,
            check_vma=False,
        )(*arrays)

    return layer
```
